128 devices in a mesh: row: 8 (over y, core), col: 16 (over z, x).
Axes of the slice: x: 4, y: 4, z: 4, core: 2. Of those that a mesh axis runs over, the one named last changes fastest.
Arguments:
- gradient: bfloat16 [8192, 14784], P(('row', 'col')), may hold values from -6 to 6
- momentum: float32 [8192, 14784], P('row', 'col'), may hold values from -6 to 6
- basis: float32 [14784, 512], P('col'), may hold values from -0.046875 to 0.046875
Outputs:
- update: bfloat16 [8192, 14784], P(('row', 'col'))
- new_momentum: float32 [8192, 14784], P('row', 'col')
- new_basis: float32 [14784, 512], P('col')
The draws below stay inside these ranges and needn't reach their ends.
All inputs are finite; a program needn't handle non-finite values.
Results may differ from the reference program's by a relative error of at most 0.001.
Values may be sent and summed in bfloat16 or wider, within the bound.
No kernel may reach another device: no remote copies, remote signals or barrier semaphores. Data moves between devices by JAX's collectives and lax.ppermute only.
A program may use at most 128 MiB of HBM per device.

```python
import jax
import jax.numpy as jnp
from jax import lax

D = 8192
FF = 14784
RANK = 512


def shard_levels(key, extent, split, smallest, top_value):
    factor_of, own = 1.0, jax.random.fold_in(key, 6)
    for dim, shards_of in split:
        draws = jnp.exp(jax.random.uniform(jax.random.fold_in(own, dim), (shards_of,), jnp.float32, smallest / len(split), top_value / len(split)))
        factor_of = factor_of * jnp.repeat(draws, extent[dim] // shards_of).reshape([-1 if axis == dim else 1 for axis in range(len(extent))])
    return factor_of


def bell_draw(key, extent, deviation, most, pieces=(), kind=jnp.bfloat16):
    loudness = shard_levels(key, extent, pieces, -0.22, 0.18) if pieces else 1.0
    entries = jax.random.normal(key, extent, jnp.float32) * deviation * loudness
    return jnp.minimum(jnp.maximum(entries, -most), most).astype(kind)


def setup_inputs(seed: int = 0) -> dict:
    keys = jax.random.split(jax.random.key(seed), 4)
    gradient = bell_draw(keys[0], (D, FF), 1.0, 6.0, ((0, 128),))
    momentum = bell_draw(keys[1], (D, FF), 1.0, 6.0, ((0, 8), (1, 16)), jnp.float32)
    basis = bell_draw(keys[2], (FF, RANK), FF ** -0.5, 0.046875, ((0, 16),), jnp.float32)
    return dict(gradient=gradient, momentum=momentum, basis=basis)


feedback_keep = 0.05
epsilon = 1e-06

def reference(gradient, momentum, basis):
    highest = lax.Precision.HIGHEST
    summed = momentum + gradient.astype(jnp.float32)
    projected = jnp.dot(summed, basis, precision=highest)
    gram_matrix = jnp.dot(projected.T, projected, precision=highest)
    lower_factor = jnp.linalg.cholesky(gram_matrix)
    orthonormal = jax.scipy.linalg.solve_triangular(lower_factor, projected.T, lower=True).T
    right_factor = jnp.dot(summed.T, orthonormal, precision=highest)
    squares = lax.optimization_barrier(jnp.sum(right_factor * right_factor, axis=0))
    new_basis = right_factor * lax.rsqrt(squares + epsilon)
    new_momentum = summed - feedback_keep * jnp.dot(orthonormal, right_factor.T, precision=highest)
    scaling = (D * FF / RANK) ** 0.5
    update = (scaling * jnp.dot(orthonormal, new_basis.T, precision=highest)).astype(jnp.bfloat16)
    return (update, new_momentum, new_basis)
```

```python
import functools

import jax
import jax.numpy as jnp
from jax import lax
from jax.experimental import pallas as pl
from jax.experimental.pallas import tpu as pltpu
from jax.sharding import Mesh, PartitionSpec as P

D = 8192
FF = 14784
RANK = 512
NB = 128

feedback_keep = 0.05
epsilon = 1e-06

HIGHEST = lax.Precision.HIGHEST
HIGH = lax.Precision.HIGH


def split3(x):
    a = x.astype(jnp.bfloat16)
    r = x - a.astype(jnp.float32)
    b = r.astype(jnp.bfloat16)
    c = (r - b.astype(jnp.float32)).astype(jnp.bfloat16)
    return [t.astype(jnp.float32) for t in (a, b, c)]


def outer8(u, v):
    a1, a2, a3 = split3(u)
    b1, b2, b3 = split3(v)
    ul = jnp.concatenate([a1, a1, a2, a2, a1, a3], 0).astype(jnp.bfloat16)
    vl = jnp.concatenate([b1, b2, b1, b2, b3, b1], 0).astype(jnp.bfloat16)
    return lax.dot_general(
        ul, vl, (((0,), (0,)), ((), ())), preferred_element_type=jnp.float32
    )


def panel(rows, p):
    lane = lax.broadcasted_iota(jnp.int32, (8, NB), 1)
    sub = lax.broadcasted_iota(jnp.int32, (8, NB), 0)
    inv = jnp.where(lane == sub + 8 * p, 1.0, 0.0).astype(jnp.float32)
    bc = [jnp.broadcast_to(rows[:, 8 * p + t : 8 * p + t + 1], (8, NB)) for t in range(8)]
    for j in range(8):
        s = lax.rsqrt(jnp.broadcast_to(bc[j][j : j + 1, :], (8, NB)))
        m = jnp.where(sub > j, bc[j] * s, 0.0)

        def step(x):
            u = jnp.broadcast_to(x[j : j + 1, :], (8, NB)) * s
            return jnp.where(sub == j, u, x - m * u)

        for t in range(j + 1, 8):
            bc[t] = step(bc[t])
        rows = step(rows)
        inv = step(inv)
    new = jnp.where((lane >= 8 * p) & (lane < 8 * p + 8), inv, rows)
    mult = jnp.where(lane >= 8 * p + 8, rows, 0.0)
    return new, mult


def block(c_ref):
    for p in range(NB // 8):
        new, mult = panel(c_ref[8 * p : 8 * p + 8, :], p)
        c_ref[8 * p : 8 * p + 8, :] = new
        if p < NB // 8 - 1:
            lo = 8 * p + 8
            upd = outer8(mult, new)[lo:, :]
            lane = lax.broadcasted_iota(jnp.int32, (NB - lo, NB), 1)
            cur = c_ref[lo:, :]
            cur = jnp.where((lane >= 8 * p) & (lane < 8 * p + 8), 0.0, cur)
            c_ref[lo:, :] = cur - upd
    r = lax.broadcasted_iota(jnp.int32, (NB, NB), 0)
    c = lax.broadcasted_iota(jnp.int32, (NB, NB), 1)
    return jnp.where(r >= c, c_ref[...], 0.0)


def inverse_kernel(n, g_ref, o_ref, c_ref):
    nb = n // NB
    o_ref[...] = g_ref[...]
    for k in range(nb):
        a, b = k * NB, (k + 1) * NB
        c_ref[...] = o_ref[a:b, a:b]
        x = block(c_ref)
        row = jnp.dot(x, o_ref[a:b, :], precision=HIGHEST, preferred_element_type=jnp.float32)
        lane = lax.broadcasted_iota(jnp.int32, (NB, n), 1)
        row = jnp.where((lane >= a) & (lane < b), jnp.concatenate([x] * nb, 1), row)
        o_ref[a:b, :] = jnp.where(lane < b, row, 0.0)
        if k < nb - 1:
            upd = lax.dot_general(
                row[:, b:],
                row,
                (((0,), (0,)), ((), ())),
                precision=HIGHEST,
                preferred_element_type=jnp.float32,
            )
            lane = lax.broadcasted_iota(jnp.int32, (n - b, n), 1)
            cur = jnp.where((lane >= a) & (lane < b), 0.0, o_ref[b:, :])
            o_ref[b:, :] = cur - upd


def inverse_factor(g):
    n = g.shape[0]
    return pl.pallas_call(
        functools.partial(inverse_kernel, n),
        out_shape=jax.ShapeDtypeStruct((n, n), jnp.float32),
        in_specs=[pl.BlockSpec(memory_space=pltpu.VMEM)],
        out_specs=pl.BlockSpec(memory_space=pltpu.VMEM),
        scratch_shapes=[pltpu.VMEM((NB, NB), jnp.float32)],
        compiler_params=pltpu.CompilerParams(vmem_limit_bytes=32 * 1024 * 1024),
        cost_estimate=pl.CostEstimate(
            flops=16 * 10**9, bytes_accessed=2 * n * n * 4, transcendentals=n
        ),
        name="inverse_factor",
    )(g)


def shift(x, axis, d, n=4):
    return lax.ppermute(x, axis, [(i, (i + d) % n) for i in range(n)])


def pick(x, axis, d):
    return lax.dynamic_index_in_dim(x, (lax.axis_index(axis) + d) % 4, 0, False)


def ring_scatter(x, axis):
    half = x.shape[1] // 2
    far = pick(x, axis, 2)
    from_prev = shift(far[:half], axis, 1)
    from_next = shift(far[half:], axis, -1)
    up, down = pick(x, axis, 1), pick(x, axis, 3)
    up = jnp.concatenate([up[:half] + from_prev, up[half:]], 0)
    down = jnp.concatenate([down[:half], down[half:] + from_next], 0)
    return pick(x, axis, 0) + shift(up, axis, 1) + shift(down, axis, -1)


def arrange(parts, axis):
    me = lax.axis_index(axis)
    out = jnp.zeros((4,) + parts[0].shape, parts[0].dtype)
    for d, part in enumerate(parts):
        out = lax.dynamic_update_index_in_dim(out, part, (me + d) % 4, 0)
    return out


def ring_gather(x, axis):
    half = x.shape[0] // 2
    prev, nxt = shift(x, axis, 1), shift(x, axis, -1)
    far = jnp.concatenate([shift(prev[:half], axis, 1), shift(nxt[half:], axis, -1)], 0)
    return arrange([x, nxt, far, prev], axis)


def direct_gather(x, axis):
    return arrange([x, shift(x, axis, -1), shift(x, axis, 2), shift(x, axis, 1)], axis)


def direct_sum(x, axis):
    return x + shift(x, axis, -1) + shift(x, axis, 2) + shift(x, axis, 1)


def other_core(x):
    return lax.ppermute(x, "c", [(0, 1), (1, 0)])


def reduce_projected(partial):
    rows, cols = partial.shape
    a, b = partial[:, : cols // 2], partial[:, cols // 2 :]
    w = cols // 2
    a = ring_scatter(a.reshape(4, rows // 4, w), "z")
    a = ring_scatter(a.reshape(4, rows // 16, w), "x")
    b = b.reshape(4, 4, rows // 16, w).transpose(1, 0, 2, 3).reshape(4, rows // 4, w)
    b = ring_scatter(b, "x")
    b = ring_scatter(b.reshape(4, rows // 16, w), "z")
    a = ring_gather(a, "x").reshape(rows // 4, w)
    a = ring_gather(a, "z").reshape(rows, w)
    b = ring_gather(b, "z").reshape(rows // 4, w)
    b = ring_gather(b, "x").reshape(4, 4, rows // 16, w).transpose(1, 0, 2, 3).reshape(rows, w)
    return jnp.concatenate([a, b], 1)


def gram_of(projected):
    n = projected.shape[1]
    slab = n // 16
    where = (lax.axis_index("z") * 4 + lax.axis_index("x")) * slab
    mine = lax.dynamic_slice_in_dim(projected, where, slab, 1)
    part = lax.dot_general(mine, projected, (((0,), (0,)), ((), ())), precision=HIGHEST)
    part = part + other_core(part)
    part = direct_sum(part, "y")
    core = lax.axis_index("c")
    half = lax.dynamic_slice_in_dim(part, core * (n // 2), n // 2, 1)
    half = direct_gather(half, "x").reshape(4 * slab, n // 2)
    half = direct_gather(half, "z").reshape(n, n // 2)
    theirs = other_core(half)
    left = jnp.where(core == 0, half, theirs)
    right = jnp.where(core == 0, theirs, half)
    return jnp.concatenate([left, right], 1)


def sum_over_row(w):
    rows, cols = w.shape
    core = lax.axis_index("c")
    left, right = w[:, : cols // 2], w[:, cols // 2 :]
    mine = jnp.where(core == 0, left, right)
    mine = mine + other_core(jnp.where(core == 0, right, left))
    part = ring_scatter(mine.reshape(4, rows // 4, cols // 2), "y")
    mine = ring_gather(part, "y").reshape(rows, cols // 2)
    theirs = other_core(mine)
    left = jnp.where(core == 0, mine, theirs)
    right = jnp.where(core == 0, theirs, mine)
    return jnp.concatenate([left, right], 1)


def local(gradient, momentum, basis):
    cols = momentum.shape[1]
    padded = -(-cols // 32) * 32
    grad_tiles = lax.all_to_all(gradient, ("z", "x"), split_axis=1, concat_axis=0, tiled=True)
    summed = momentum + grad_tiles.astype(jnp.float32)
    projected = reduce_projected(jnp.dot(summed, basis, precision=HIGH))
    mixed = lax.dot_general(summed, projected, (((0,), (0,)), ((), ())), precision=HIGH)
    mixed = sum_over_row(jnp.pad(mixed, ((0, padded - cols), (0, 0))))[:cols]
    inverse = inverse_factor(gram_of(projected))
    contract = (((1,), (1,)), ((), ()))
    orthonormal = lax.dot_general(projected, inverse, contract, precision=HIGH)
    right_factor = lax.dot_general(mixed, inverse, contract, precision=HIGH)
    squares = jnp.sum(right_factor * right_factor, axis=0, keepdims=True)
    squares = direct_sum(direct_sum(jnp.broadcast_to(squares, (8, RANK)), "z"), "x")[:1]
    new_basis = right_factor * lax.rsqrt(squares + epsilon)
    new_momentum = summed - feedback_keep * lax.dot_general(
        orthonormal, right_factor, contract, precision=HIGH
    )
    scaling = (D * FF / RANK) ** 0.5
    update_tile = (
        scaling * lax.dot_general(orthonormal, new_basis, contract, precision=HIGH)
    ).astype(jnp.bfloat16)
    update = lax.all_to_all(update_tile, ("z", "x"), split_axis=0, concat_axis=1, tiled=True)
    return (update, new_momentum, new_basis)


def solution(mesh):
    fine = Mesh(mesh.devices.reshape(4, 2, 4, 4), ("y", "c", "z", "x"))
    row, col = ("y", "c"), ("z", "x")
    return jax.shard_map(
        local,
        mesh=fine,
        in_specs=(P(row + col, None), P(row, col), P(col, None)),
        out_specs=(P(row + col, None), P(row, col), P(col, None)),
        check_vma=False,
    )
```

```python
import functools

import jax
import jax.numpy as jnp
from jax import lax
from jax.experimental import pallas as pl
from jax.experimental.pallas import tpu as pltpu
from jax.sharding import Mesh, PartitionSpec as P

D = 8192
FF = 14784
RANK = 512
NB = 128

feedback_keep = 0.05
epsilon = 1e-06

HIGHEST = lax.Precision.HIGHEST
HIGH = lax.Precision.HIGH


def split3(x):
    a = x.astype(jnp.bfloat16)
    r = x - a.astype(jnp.float32)
    b = r.astype(jnp.bfloat16)
    c = (r - b.astype(jnp.float32)).astype(jnp.bfloat16)
    return [t.astype(jnp.float32) for t in (a, b, c)]


def outer8(u, v):
    a1, a2, a3 = split3(u)
    b1, b2, b3 = split3(v)
    ul = jnp.concatenate([a1, a1, a2, a2, a1, a3], 0).astype(jnp.bfloat16)
    vl = jnp.concatenate([b1, b2, b1, b2, b3, b1], 0).astype(jnp.bfloat16)
    return lax.dot_general(
        ul, vl, (((0,), (0,)), ((), ())), preferred_element_type=jnp.float32
    )


def panel(rows, p):
    lane = lax.broadcasted_iota(jnp.int32, (8, NB), 1)
    sub = lax.broadcasted_iota(jnp.int32, (8, NB), 0)
    inv = jnp.where(lane == sub + 8 * p, 1.0, 0.0).astype(jnp.float32)
    bc = [jnp.broadcast_to(rows[:, 8 * p + t : 8 * p + t + 1], (8, NB)) for t in range(8)]
    for j in range(8):
        s = lax.rsqrt(jnp.broadcast_to(bc[j][j : j + 1, :], (8, NB)))
        m = jnp.where(sub > j, bc[j] * s, 0.0)

        def step(x):
            u = jnp.broadcast_to(x[j : j + 1, :], (8, NB)) * s
            return jnp.where(sub == j, u, x - m * u)

        for t in range(j + 1, 8):
            bc[t] = step(bc[t])
        rows = step(rows)
        inv = step(inv)
    new = jnp.where((lane >= 8 * p) & (lane < 8 * p + 8), inv, rows)
    mult = jnp.where(lane >= 8 * p + 8, rows, 0.0)
    return new, mult


def block(c_ref):
    for p in range(NB // 8):
        new, mult = panel(c_ref[8 * p : 8 * p + 8, :], p)
        c_ref[8 * p : 8 * p + 8, :] = new
        if p < NB // 8 - 1:
            lo = 8 * p + 8
            upd = outer8(mult, new)[lo:, :]
            lane = lax.broadcasted_iota(jnp.int32, (NB - lo, NB), 1)
            cur = c_ref[lo:, :]
            cur = jnp.where((lane >= 8 * p) & (lane < 8 * p + 8), 0.0, cur)
            c_ref[lo:, :] = cur - upd
    r = lax.broadcasted_iota(jnp.int32, (NB, NB), 0)
    c = lax.broadcasted_iota(jnp.int32, (NB, NB), 1)
    return jnp.where(r >= c, c_ref[...], 0.0)


def inverse_kernel(n, k, g_ref, o_ref, c_ref):
    a, b = k * NB, (k + 1) * NB
    c_ref[...] = g_ref[a:b, a:b]
    x = block(c_ref)
    row = jnp.dot(x, g_ref[a:b, :], precision=HIGHEST, preferred_element_type=jnp.float32)
    lane = lax.broadcasted_iota(jnp.int32, (NB, n), 1)
    row = jnp.where((lane >= a) & (lane < b), jnp.concatenate([x] * (n // NB), 1), row)
    if k > 0:
        o_ref[:a, :] = g_ref[:a, :]
    o_ref[a:b, :] = jnp.where(lane < b, row, 0.0)
    if b < n:
        upd = lax.dot_general(
            row[:, b:],
            row,
            (((0,), (0,)), ((), ())),
            precision=HIGHEST,
            preferred_element_type=jnp.float32,
        )
        lane = lax.broadcasted_iota(jnp.int32, (n - b, n), 1)
        cur = jnp.where((lane >= a) & (lane < b), 0.0, g_ref[b:, :])
        o_ref[b:, :] = cur - upd


def inverse_step(g, k):
    n = g.shape[0]
    return pl.pallas_call(
        functools.partial(inverse_kernel, n, k),
        out_shape=jax.ShapeDtypeStruct((n, n), jnp.float32),
        in_specs=[pl.BlockSpec(memory_space=pltpu.VMEM)],
        out_specs=pl.BlockSpec(memory_space=pltpu.VMEM),
        scratch_shapes=[pltpu.VMEM((NB, NB), jnp.float32)],
        compiler_params=pltpu.CompilerParams(vmem_limit_bytes=32 * 1024 * 1024),
        cost_estimate=pl.CostEstimate(
            flops=6 * 10**9, bytes_accessed=2 * n * n * 4, transcendentals=n
        ),
        name="inverse_step",
    )(g)


def cut_kernel(width, x_ref, o_ref):
    for j in range(o_ref.shape[0]):
        o_ref[j] = x_ref[:, j * width : (j + 1) * width]


def cut_columns(x, parts):
    rows, width = x.shape[0], x.shape[1] // parts
    return pl.pallas_call(
        functools.partial(cut_kernel, width),
        grid=(rows // 16,),
        in_specs=[pl.BlockSpec((16, parts * width), lambda i: (i, 0))],
        out_specs=pl.BlockSpec((parts, 16, width), lambda i: (0, i, 0)),
        out_shape=jax.ShapeDtypeStruct((parts, rows, width), x.dtype),
        cost_estimate=pl.CostEstimate(
            flops=0, bytes_accessed=4 * rows * parts * width, transcendentals=0
        ),
        name="cut_columns",
    )(x)


def join_kernel(width, x_ref, o_ref):
    for j in range(x_ref.shape[0]):
        o_ref[:, j * width : (j + 1) * width] = x_ref[j]


def join_columns(x):
    parts, rows, width = x.shape
    return pl.pallas_call(
        functools.partial(join_kernel, width),
        grid=(rows // 16,),
        in_specs=[pl.BlockSpec((parts, 16, width), lambda i: (0, i, 0))],
        out_specs=pl.BlockSpec((16, parts * width), lambda i: (i, 0)),
        out_shape=jax.ShapeDtypeStruct((rows, parts * width), x.dtype),
        cost_estimate=pl.CostEstimate(
            flops=0, bytes_accessed=4 * rows * parts * width, transcendentals=0
        ),
        name="join_columns",
    )(x)


def split2(x):
    hi = x.astype(jnp.bfloat16)
    return hi, (x - hi.astype(jnp.float32)).astype(jnp.bfloat16)


def dot3(a, b):
    f32 = jnp.float32
    return (
        jnp.dot(a[0], b[0], preferred_element_type=f32)
        + jnp.dot(a[0], b[1], preferred_element_type=f32)
        + jnp.dot(a[1], b[0], preferred_element_type=f32)
    )


def add_project_kernel(g_ref, m_ref, b_ref, s_ref, p_ref, hi_ref, lo_ref):
    @pl.when(pl.program_id(0) == 0)
    def _():
        hi_ref[...], lo_ref[...] = split2(b_ref[...])

    summed = m_ref[...] + g_ref[...].astype(jnp.float32)
    s_ref[...] = summed
    p_ref[...] = dot3(split2(summed), (hi_ref[...], lo_ref[...]))


def add_project(grad, momentum, basis):
    rows, cols = momentum.shape
    rank = basis.shape[1]
    step = 256
    return pl.pallas_call(
        add_project_kernel,
        grid=(rows // step,),
        in_specs=[
            pl.BlockSpec((step, cols), lambda i: (i, 0)),
            pl.BlockSpec((step, cols), lambda i: (i, 0)),
            pl.BlockSpec((cols, rank), lambda i: (0, 0)),
        ],
        out_specs=[
            pl.BlockSpec((step, cols), lambda i: (i, 0)),
            pl.BlockSpec((step, rank), lambda i: (i, 0)),
        ],
        out_shape=[
            jax.ShapeDtypeStruct((rows, cols), jnp.float32),
            jax.ShapeDtypeStruct((rows, rank), jnp.float32),
        ],
        scratch_shapes=[pltpu.VMEM((cols, rank), jnp.bfloat16)] * 2,
        compiler_params=pltpu.CompilerParams(vmem_limit_bytes=40 * 1024 * 1024),
        cost_estimate=pl.CostEstimate(
            flops=6 * rows * cols * rank, bytes_accessed=10 * rows * cols, transcendentals=0
        ),
        name="add_project",
    )(grad, momentum, basis)


def shift(x, axis, d, n=4):
    return lax.ppermute(x, axis, [(i, (i + d) % n) for i in range(n)])


def other_core(x):
    return lax.ppermute(x, "c", [(0, 1), (1, 0)])


def partners(axis):
    i = lax.axis_index(axis)
    first = lax.axis_index("c") == 0
    one, two = jnp.bitwise_xor(i, 1), 3 - i
    return i, jnp.where(first, one, two), jnp.where(first, two, one), jnp.bitwise_xor(i, 2)


def swap(x, axis, turn):
    perm = []
    for c in range(2):
        for i in range(4):
            j = i ^ 1 if c == turn else 3 - i
            perm.append((2 * i + c, 2 * j + c) if axis == "y" else (4 * c + i, 4 * c + j))
    return lax.ppermute(x, ("y", "c") if axis == "y" else ("c", axis), perm)


def pick(x, i):
    return lax.dynamic_index_in_dim(x, i, 0, False)


def pair_scatter_start(x, axis):
    i, p1, p2, far = partners(axis)
    got = swap(jnp.stack([pick(x, p1), pick(x, far)]), axis, 0)
    return pick(x, i) + got[0], pick(x, p2) + got[1]


def pair_scatter_end(both, axis):
    return both[0] + swap(both[1], axis, 1)


def pair_scatter(x, axis):
    return pair_scatter_end(pair_scatter_start(x, axis), axis)


def pair_gather_start(x, axis):
    return jnp.stack([x, swap(x, axis, 1)])


def pair_gather(x, axis):
    return pair_gather_end(pair_gather_start(x, axis), axis)


def pair_gather_end(two, axis):
    i, p1, p2, far = partners(axis)
    x = two[0]
    got = swap(two, axis, 0)
    out = jnp.zeros((4,) + x.shape, x.dtype)
    for where, part in ((i, two[0]), (p2, two[1]), (p1, got[0]), (far, got[1])):
        out = lax.dynamic_update_index_in_dim(out, part, where, 0)
    return out


def pair_sum(x, axis):
    x = x + swap(x, axis, 0)
    return x + swap(x, axis, 1)


def direct_gather(x, axis):
    me = lax.axis_index(axis)
    out = jnp.zeros((4,) + x.shape, x.dtype)
    for d, part in ((0, x), (3, shift(x, axis, 1)), (2, shift(x, axis, 2)), (1, shift(x, axis, 3))):
        out = lax.dynamic_update_index_in_dim(out, part, (me + d) % 4, 0)
    return out


def direct_sum(x, axis):
    return (x + shift(x, axis, 2)) + (shift(x, axis, 1) + shift(x, axis, 3))


def reduce_projected(partial):
    rows, cols = partial.shape
    w = cols // 2
    a = partial[:, :w].reshape(4, rows // 4, w)
    b = partial[:, w:].reshape(4, rows // 4, w)
    a, b = pair_scatter(a, "z"), pair_scatter(b, "x")
    a, b = pair_sum(a, "x"), pair_sum(b, "z")
    a, b = pair_gather(a, "z"), pair_gather(b, "x")
    return jnp.concatenate([a.reshape(rows, w), b.reshape(rows, w)], 1)


def both_halves(mine):
    first = lax.axis_index("c") == 0
    theirs = other_core(mine)
    return jnp.concatenate([jnp.where(first, mine, theirs), jnp.where(first, theirs, mine)], 1)


def core_scatter(x):
    first = lax.axis_index("c") == 0
    left, right = jnp.split(x, 2, axis=1)
    return jnp.where(first, left, right) + other_core(jnp.where(first, right, left))


def row_end(parts, axis):
    return both_halves(parts.reshape(-1, parts.shape[2]))


def gram_slab(projected):
    slab = projected.shape[1] // 4
    mine = lax.dynamic_slice_in_dim(projected, lax.axis_index("z") * slab, slab, 1)
    return lax.dot_general(mine, projected, (((0,), (0,)), ((), ())), precision=HIGHEST)


def gram_sum(part):
    n = part.shape[1]
    part = direct_sum(core_scatter(part), "y")
    return both_halves(direct_gather(part, "z").reshape(n, n // 2))


def local(gradient, momentum, basis):
    rows, cols = momentum.shape
    pieces = lax.all_to_all(cut_columns(gradient, 16), ("z", "x"), 0, 0, tiled=True)
    summed, partial = add_project(pieces.reshape(rows, cols), momentum, basis)
    projected = reduce_projected(partial)
    slab, projected = lax.optimization_barrier((gram_slab(projected), projected))
    mixed = lax.dot_general(summed, projected, (((0,), (0,)), ((), ())), precision=HIGH)
    mixed = core_scatter(jnp.pad(mixed, ((0, -cols % 32), (0, 0))))
    mixed = pair_scatter_start(mixed.reshape(4, -1, RANK // 2), "y")
    inverse = gram_sum(slab)
    for k, stage in enumerate((pair_scatter_end, pair_gather_start, pair_gather_end, row_end)):
        inverse, mixed = lax.optimization_barrier((inverse, mixed))
        inverse, mixed = inverse_step(inverse, k), stage(mixed, "y")
    mixed = mixed[:cols]
    contract = (((1,), (1,)), ((), ()))
    orthonormal = lax.dot_general(projected, inverse, contract, precision=HIGH)
    right_factor = lax.dot_general(mixed, inverse, contract, precision=HIGH)
    squares = jnp.sum(right_factor * right_factor, axis=0, keepdims=True)
    squares = direct_sum(direct_sum(jnp.broadcast_to(squares, (8, RANK)), "z"), "x")[:1]
    new_basis = right_factor * lax.rsqrt(squares + epsilon)
    new_momentum = summed - feedback_keep * lax.dot_general(
        orthonormal, right_factor, contract, precision=HIGH
    )
    scaling = (D * FF / RANK) ** 0.5
    update_tile = (
        scaling * lax.dot_general(orthonormal, new_basis, contract, precision=HIGH)
    ).astype(jnp.bfloat16)
    pieces = lax.all_to_all(update_tile.reshape(16, rows // 16, cols), ("z", "x"), 0, 0, tiled=True)
    return (join_columns(pieces), new_momentum, new_basis)


def solution(mesh):
    fine = Mesh(mesh.devices.reshape(4, 2, 4, 4), ("y", "c", "z", "x"))
    row, col = ("y", "c"), ("z", "x")
    return jax.shard_map(
        local,
        mesh=fine,
        in_specs=(P(row + col, None), P(row, col), P(col, None)),
        out_specs=(P(row + col, None), P(row, col), P(col, None)),
        check_vma=False,
    )
```

```python
import functools

import jax
import jax.numpy as jnp
from jax import lax
from jax.experimental import pallas as pl
from jax.experimental.pallas import tpu as pltpu
from jax.sharding import Mesh, PartitionSpec as P

D = 8192
FF = 14784
RANK = 512
NB = 128
PANEL = 16

feedback_keep = 0.05
epsilon = 1e-06

HIGHEST = lax.Precision.HIGHEST
HIGH = lax.Precision.HIGH


def split3(x):
    a = x.astype(jnp.bfloat16)
    r = x - a.astype(jnp.float32)
    b = r.astype(jnp.bfloat16)
    c = (r - b.astype(jnp.float32)).astype(jnp.bfloat16)
    return [t.astype(jnp.float32) for t in (a, b, c)]


def outer(u, v):
    a1, a2, a3 = split3(u)
    b1, b2, b3 = split3(v)
    ul = jnp.concatenate([a1, a1, a2, a2, a1, a3], 0).astype(jnp.bfloat16)
    vl = jnp.concatenate([b1, b2, b1, b2, b3, b1], 0).astype(jnp.bfloat16)
    return lax.dot_general(
        ul, vl, (((0,), (0,)), ((), ())), preferred_element_type=jnp.float32
    )


def panel(rows, p):
    base = PANEL * p
    tiles = PANEL // 8
    lane = lax.broadcasted_iota(jnp.int32, (8, NB), 1)
    sub = lax.broadcasted_iota(jnp.int32, (8, NB), 0)
    inv = [jnp.where(lane == sub + base + 8 * q, 1.0, 0.0).astype(jnp.float32) for q in range(tiles)]
    bc = [
        [jnp.broadcast_to(rows[q][:, base + t : base + t + 1], (8, NB)) for q in range(tiles)]
        for t in range(PANEL)
    ]
    scale = [None] * tiles
    for j in range(PANEL):
        k, r = divmod(j, 8)
        s = lax.rsqrt(jnp.broadcast_to(bc[j][k][r : r + 1, :], (8, NB)))
        scale[k] = s if r == 0 else jnp.where(sub == r, s, scale[k])
        m = [(bc[j][q] * s) * s for q in range(tiles)]
        m[k] = jnp.where(sub > r, m[k], 0.0)

        def step(v):
            u = jnp.broadcast_to(v[k][r : r + 1, :], (8, NB))
            return [v[q] - m[q] * u if q >= k else v[q] for q in range(tiles)]

        for t in range(j + 1, PANEL):
            bc[t] = step(bc[t])
        rows = step(rows)
        inv = step(inv)
    inside = (lane >= base) & (lane < base + PANEL)
    new = [jnp.where(inside, inv[q], rows[q]) * scale[q] for q in range(tiles)]
    mult = [jnp.where(lane >= base + PANEL, new[q], 0.0) for q in range(tiles)]
    return new, mult


def block(x):
    n, tiles = NB // 8, PANEL // 8
    t = [x[8 * q : 8 * q + 8, :] for q in range(n)]
    lane = lax.broadcasted_iota(jnp.int32, (8, NB), 1)
    for p in range(NB // PANEL):
        lo, hi = tiles * p, tiles * (p + 1)
        new, mult = panel(t[lo:hi], p)
        t[lo:hi] = new
        if hi < n:
            upd = outer(jnp.concatenate(mult, 0), jnp.concatenate(new, 0))
            keep = (lane < PANEL * p) | (lane >= PANEL * (p + 1))
            for q in range(hi, n):
                t[q] = jnp.where(keep, t[q], 0.0) - upd[8 * q : 8 * q + 8, :]
    r = lax.broadcasted_iota(jnp.int32, (NB, NB), 0)
    c = lax.broadcasted_iota(jnp.int32, (NB, NB), 1)
    return jnp.where(r >= c, jnp.concatenate(t, 0), 0.0)


def inverse_kernel(n, k, g_ref, o_ref):
    a, b = k * NB, (k + 1) * NB
    x = block(g_ref[a:b, a:b])
    row = jnp.dot(x, g_ref[a:b, :], precision=HIGHEST, preferred_element_type=jnp.float32)
    lane = lax.broadcasted_iota(jnp.int32, (NB, n), 1)
    row = jnp.where((lane >= a) & (lane < b), jnp.concatenate([x] * (n // NB), 1), row)
    if k > 0:
        o_ref[:a, :] = g_ref[:a, :]
    o_ref[a:b, :] = jnp.where(lane < b, row, 0.0)
    if b < n:
        upd = lax.dot_general(
            row[:, b:],
            row,
            (((0,), (0,)), ((), ())),
            precision=HIGHEST,
            preferred_element_type=jnp.float32,
        )
        lane = lax.broadcasted_iota(jnp.int32, (n - b, n), 1)
        cur = jnp.where((lane >= a) & (lane < b), 0.0, g_ref[b:, :])
        o_ref[b:, :] = cur - upd


def inverse_step(g, k):
    n = g.shape[0]
    return pl.pallas_call(
        functools.partial(inverse_kernel, n, k),
        out_shape=jax.ShapeDtypeStruct((n, n), jnp.float32),
        in_specs=[pl.BlockSpec(memory_space=pltpu.VMEM)],
        out_specs=pl.BlockSpec(memory_space=pltpu.VMEM),
        compiler_params=pltpu.CompilerParams(vmem_limit_bytes=32 * 1024 * 1024),
        cost_estimate=pl.CostEstimate(
            flops=4 * 10**9, bytes_accessed=2 * n * n * 4, transcendentals=n
        ),
        name="inverse_step",
    )(g)


def pack(piece):
    rows, width = piece.shape
    whole = width // 128
    rest = piece[:, whole * 128 :]
    quarter = rows // 4
    side = [rest[q * quarter : (q + 1) * quarter] for q in range(4)]
    side.append(jnp.zeros((quarter, 128 - 4 * (width % 128)), piece.dtype))
    tiles = [piece[:, t * 128 : (t + 1) * 128] for t in range(whole)]
    return jnp.concatenate(tiles + [jnp.concatenate(side, 1)], 0)


def unpack(packed, rows, width):
    whole, left, quarter = width // 128, width % 128, rows // 4
    tiles = [packed[t * rows : (t + 1) * rows] for t in range(whole)]
    side = packed[whole * rows :]
    tiles.append(jnp.concatenate([side[:, q * left : (q + 1) * left] for q in range(4)], 0))
    return jnp.concatenate(tiles, 1)


def packed_rows(rows, width):
    return rows * (width // 128) + rows // 4


def cut_kernel(width, x_ref, o_ref):
    for j in range(o_ref.shape[0]):
        o_ref[j] = pack(x_ref[:, j * width : (j + 1) * width])


def cut_columns(x, parts):
    rows, width = x.shape[0], x.shape[1] // parts
    shape = (parts, packed_rows(rows, width), 128)
    return pl.pallas_call(
        functools.partial(cut_kernel, width),
        in_specs=[pl.BlockSpec(memory_space=pltpu.VMEM)],
        out_specs=pl.BlockSpec(memory_space=pltpu.VMEM),
        out_shape=jax.ShapeDtypeStruct(shape, x.dtype),
        compiler_params=pltpu.CompilerParams(vmem_limit_bytes=32 * 1024 * 1024),
        cost_estimate=pl.CostEstimate(
            flops=0, bytes_accessed=4 * rows * parts * width, transcendentals=0
        ),
        name="cut_columns",
    )(x)


def join_kernel(width, x_ref, o_ref):
    for j in range(x_ref.shape[0]):
        o_ref[:, j * width : (j + 1) * width] = unpack(x_ref[j], o_ref.shape[0], width)


def join_columns(x, rows, width):
    parts = x.shape[0]
    return pl.pallas_call(
        functools.partial(join_kernel, width),
        in_specs=[pl.BlockSpec(memory_space=pltpu.VMEM)],
        out_specs=pl.BlockSpec(memory_space=pltpu.VMEM),
        out_shape=jax.ShapeDtypeStruct((rows, parts * width), x.dtype),
        compiler_params=pltpu.CompilerParams(vmem_limit_bytes=32 * 1024 * 1024),
        cost_estimate=pl.CostEstimate(
            flops=0, bytes_accessed=4 * rows * parts * width, transcendentals=0
        ),
        name="join_columns",
    )(x)


def split2(x):
    hi = x.astype(jnp.bfloat16)
    return hi, (x - hi.astype(jnp.float32)).astype(jnp.bfloat16)


def dot3(a, b):
    f32 = jnp.float32
    return (
        jnp.dot(a[0], b[0], preferred_element_type=f32)
        + jnp.dot(a[0], b[1], preferred_element_type=f32)
        + jnp.dot(a[1], b[0], preferred_element_type=f32)
    )


def add_project_kernel(slot_ref, g_ref, m_ref, b_ref, s_ref, *refs):
    hi_ref, lo_ref = refs[8:]

    @pl.when(pl.program_id(0) == 0)
    def _():
        hi_ref[...], lo_ref[...] = split2(b_ref[...])

    rows, cols = m_ref.shape
    grad = [unpack(g_ref[k], rows // 4, cols) for k in range(4)]
    summed = m_ref[...] + jnp.concatenate(grad, 0).astype(jnp.float32)
    s_ref[...] = summed
    part = dot3(split2(summed), (hi_ref[...], lo_ref[...]))
    half = part.shape[1] // 2
    for side in range(2):
        slot = slot_ref[4 * side + pl.program_id(0)]
        for to in range(4):

            @pl.when(slot == to)
            def _(side=side, to=to):
                refs[4 * side + to][...] = part[:, side * half : (side + 1) * half]


def add_project(slots, grad, momentum, basis):
    rows, cols = momentum.shape
    rank = basis.shape[1]
    step = rows // 4
    return pl.pallas_call(
        add_project_kernel,
        grid=(rows // step,),
        in_specs=[
            pl.BlockSpec(memory_space=pltpu.SMEM),
            pl.BlockSpec((4,) + grad.shape[1:], lambda i: (i, 0, 0)),
            pl.BlockSpec((step, cols), lambda i: (i, 0)),
            pl.BlockSpec((cols, rank), lambda i: (0, 0)),
        ],
        out_specs=[
            pl.BlockSpec((step, cols), lambda i: (i, 0)),
        ]
        + [pl.BlockSpec((step, rank // 2), lambda i: (0, 0))] * 8,
        out_shape=[jax.ShapeDtypeStruct((rows, cols), jnp.float32)]
        + [jax.ShapeDtypeStruct((step, rank // 2), jnp.float32)] * 8,
        scratch_shapes=[pltpu.VMEM((cols, rank), jnp.bfloat16)] * 2,
        compiler_params=pltpu.CompilerParams(vmem_limit_bytes=36 * 1024 * 1024),
        cost_estimate=pl.CostEstimate(
            flops=6 * rows * cols * rank, bytes_accessed=10 * rows * cols, transcendentals=0
        ),
        name="add_project",
    )(slots, grad, momentum, basis)


def update_kernel(scaling, q_ref, b_ref, o_ref, hi_ref, lo_ref):
    @pl.when(pl.program_id(0) == 0)
    def _():
        hi_ref[...], lo_ref[...] = split2(b_ref[...])

    q = split2(q_ref[...])
    dims = (((1,), (1,)), ((), ()))
    f32 = jnp.float32
    out = lax.dot_general(q[0], hi_ref[...], dims, preferred_element_type=f32)
    out += lax.dot_general(q[0], lo_ref[...], dims, preferred_element_type=f32)
    out += lax.dot_general(q[1], hi_ref[...], dims, preferred_element_type=f32)
    out = (scaling * out).astype(jnp.bfloat16)
    part = out.shape[0] // 4
    for k in range(4):
        o_ref[k] = pack(out[k * part : (k + 1) * part])


def update_of(orthonormal, new_basis, scaling):
    rows, rank = orthonormal.shape
    cols = new_basis.shape[0]
    step = rows // 4
    packed = packed_rows(rows // 16, cols)
    return pl.pallas_call(
        functools.partial(update_kernel, scaling),
        grid=(rows // step,),
        in_specs=[
            pl.BlockSpec((step, rank), lambda i: (i, 0)),
            pl.BlockSpec((cols, rank), lambda i: (0, 0)),
        ],
        out_specs=pl.BlockSpec((4, packed, 128), lambda i: (i, 0, 0)),
        out_shape=jax.ShapeDtypeStruct((16, packed, 128), jnp.bfloat16),
        scratch_shapes=[pltpu.VMEM((cols, rank), jnp.bfloat16)] * 2,
        compiler_params=pltpu.CompilerParams(vmem_limit_bytes=32 * 1024 * 1024),
        cost_estimate=pl.CostEstimate(
            flops=6 * rows * cols * rank, bytes_accessed=4 * rows * cols, transcendentals=0
        ),
        name="update_tile",
    )(orthonormal, new_basis)


def shift(x, axis, d, n=4):
    return lax.ppermute(x, axis, [(i, (i + d) % n) for i in range(n)])


def other_core(x):
    return lax.ppermute(x, "c", [(0, 1), (1, 0)])


def partners(axis):
    i = lax.axis_index(axis)
    first = lax.axis_index("c") == 0
    one, two = jnp.bitwise_xor(i, 1), 3 - i
    return i, jnp.where(first, one, two), jnp.where(first, two, one), jnp.bitwise_xor(i, 2)


def swap(x, axis, turn):
    perm = []
    for c in range(2):
        for i in range(4):
            j = i ^ 1 if c == turn else 3 - i
            perm.append((2 * i + c, 2 * j + c) if axis == "y" else (4 * c + i, 4 * c + j))
    return lax.ppermute(x, ("y", "c") if axis == "y" else ("c", axis), perm)


def pick(x, i):
    return lax.dynamic_index_in_dim(x, i, 0, False)


def slots_of(axis):
    i, p1, p2, far = partners(axis)
    k = jnp.arange(4, dtype=jnp.int32)
    return jnp.where(k == i, 0, jnp.where(k == p2, 1, jnp.where(k == p1, 2, 3))).astype(jnp.int32)


def pair_scatter_start(parts, axis):
    got_far = swap(parts[3], axis, 0)
    got_own = swap(parts[2], axis, 0)
    return parts[0], got_own, swap(parts[1] + got_far, axis, 1)


def pair_scatter(parts, axis):
    return sum_parts(pair_scatter_start(parts, axis))


def sum_parts(parts):
    return parts[0] + parts[1] + parts[2]


def quarters(x, axis):
    i, p1, p2, far = partners(axis)
    return [pick(x, k) for k in (i, p2, p1, far)]


def pair_gather_start(x, axis):
    return x, swap(x, axis, 1), swap(x, axis, 0)


def pair_gather_end(parts, axis):
    i, p1, p2, far = partners(axis)
    x, got2, got1 = parts
    out = jnp.zeros((4,) + x.shape, x.dtype)
    for where, part in ((i, x), (p2, got2), (p1, got1), (far, swap(got2, axis, 0))):
        out = lax.dynamic_update_index_in_dim(out, part, where, 0)
    return out


def pair_gather(x, axis):
    return pair_gather_end(pair_gather_start(x, axis), axis)


def pair_sum(x, axis):
    x = x + swap(x, axis, 0)
    return x + swap(x, axis, 1)


def direct_gather(x, axis):
    me = lax.axis_index(axis)
    out = jnp.zeros((4,) + x.shape, x.dtype)
    for d, part in ((0, x), (3, shift(x, axis, 1)), (2, shift(x, axis, 2)), (1, shift(x, axis, 3))):
        out = lax.dynamic_update_index_in_dim(out, part, (me + d) % 4, 0)
    return out


def direct_sum(x, axis):
    return (x + shift(x, axis, 2)) + (shift(x, axis, 1) + shift(x, axis, 3))


def reduce_projected(left, right):
    a, b = pair_scatter(left, "z"), pair_scatter(right, "x")
    a, b = pair_sum(a, "x"), pair_sum(b, "z")
    a, b = pair_gather(a, "z"), pair_gather(b, "x")
    rows, w = 4 * a.shape[1], a.shape[2]
    return jnp.concatenate([a.reshape(rows, w), b.reshape(rows, w)], 1)


def both_halves(mine):
    first = lax.axis_index("c") == 0
    theirs = other_core(mine)
    return jnp.concatenate([jnp.where(first, mine, theirs), jnp.where(first, theirs, mine)], 1)


def core_scatter(x):
    first = lax.axis_index("c") == 0
    left, right = jnp.split(x, 2, axis=1)
    return jnp.where(first, left, right) + other_core(jnp.where(first, right, left))


def gram_slab(projected):
    slab = projected.shape[1] // 4
    mine = lax.dynamic_slice_in_dim(projected, lax.axis_index("z") * slab, slab, 1)
    return lax.dot_general(mine, projected, (((0,), (0,)), ((), ())), precision=HIGHEST)


def gram_gather(part):
    n = 4 * part.shape[0]
    return both_halves(direct_gather(part, "z").reshape(n, n // 2))


def local(gradient, momentum, basis):
    rows, cols = momentum.shape
    pieces = lax.all_to_all(cut_columns(gradient, 16), ("z", "x"), 0, 0, tiled=True)
    slots = jnp.concatenate([slots_of("z"), slots_of("x")])
    summed, *partial = add_project(slots, pieces, momentum, basis)
    projected = reduce_projected(partial[:4], partial[4:])
    slab = gram_slab(projected)
    dims = (((0,), (0,)), ((), ()))
    half = RANK // 2
    stages = (
        (core_scatter, lambda p: lax.dot_general(summed, p, dims, precision=HIGH)),
        (
            lambda g: direct_sum(g, "y"),
            lambda w: core_scatter(jnp.pad(w, ((0, -cols % 32), (0, 0)))),
        ),
        (gram_gather, lambda w: pair_scatter(quarters(w.reshape(4, -1, half), "y"), "y")),
        (lambda g: inverse_step(g, 0), lambda w: pair_gather_start(w, "y")),
        (lambda g: inverse_step(inverse_step(g, 1), 2), lambda w: pair_gather_end(w, "y")),
        (lambda g: inverse_step(g, 3), lambda w: both_halves(w.reshape(-1, half))),
    )
    mixed = projected
    inverse = slab
    for of_gram, of_mixed in stages:
        inverse, mixed = lax.optimization_barrier((inverse, mixed))
        inverse, mixed = of_gram(inverse), of_mixed(mixed)
    mixed = mixed[:cols]
    contract = (((1,), (1,)), ((), ()))
    orthonormal = lax.dot_general(projected, inverse, contract, precision=HIGH)
    right_factor = lax.dot_general(mixed, inverse, contract, precision=HIGH)
    squares = jnp.sum(right_factor * right_factor, axis=0, keepdims=True)
    squares = direct_sum(direct_sum(jnp.broadcast_to(squares, (8, RANK)), "z"), "x")[:1]
    new_basis = right_factor * lax.rsqrt(squares + epsilon)
    new_momentum = summed - feedback_keep * lax.dot_general(
        orthonormal, right_factor, contract, precision=HIGH
    )
    scaling = (D * FF / RANK) ** 0.5
    update_tile = update_of(orthonormal, new_basis, scaling)
    pieces = lax.all_to_all(update_tile, ("z", "x"), 0, 0, tiled=True)
    return (join_columns(pieces, rows // 16, cols), new_momentum, new_basis)


def solution(mesh):
    fine = Mesh(mesh.devices.reshape(4, 2, 4, 4), ("y", "c", "z", "x"))
    row, col = ("y", "c"), ("z", "x")
    return jax.shard_map(
        local,
        mesh=fine,
        in_specs=(P(row + col, None), P(row, col), P(col, None)),
        out_specs=(P(row + col, None), P(row, col), P(col, None)),
        check_vma=False,
    )
```

```python
import functools

import jax
import jax.numpy as jnp
from jax import lax
from jax.experimental import pallas as pl
from jax.experimental.pallas import tpu as pltpu
from jax.sharding import Mesh, PartitionSpec as P

D = 8192
FF = 14784
RANK = 512
NB = 128
PANEL = 16

feedback_keep = 0.05
epsilon = 1e-06

HIGHEST = lax.Precision.HIGHEST
HIGH = lax.Precision.HIGH


def split3(x):
    a = x.astype(jnp.bfloat16)
    r = x - a.astype(jnp.float32)
    b = r.astype(jnp.bfloat16)
    c = (r - b.astype(jnp.float32)).astype(jnp.bfloat16)
    return [t.astype(jnp.float32) for t in (a, b, c)]


def outer(u, v):
    a1, a2, a3 = split3(u)
    b1, b2, b3 = split3(v)
    ul = jnp.concatenate([a1, a1, a2, a2, a1, a3], 0).astype(jnp.bfloat16)
    vl = jnp.concatenate([b1, b2, b1, b2, b3, b1], 0).astype(jnp.bfloat16)
    return lax.dot_general(
        ul, vl, (((0,), (0,)), ((), ())), preferred_element_type=jnp.float32
    )


def panel(rows, p):
    base = PANEL * p
    tiles = PANEL // 8
    lane = lax.broadcasted_iota(jnp.int32, (8, NB), 1)
    sub = lax.broadcasted_iota(jnp.int32, (8, NB), 0)
    inv = [jnp.where(lane == sub + base + 8 * q, 1.0, 0.0).astype(jnp.float32) for q in range(tiles)]
    bc = [
        [jnp.broadcast_to(rows[q][:, base + t : base + t + 1], (8, NB)) for q in range(tiles)]
        for t in range(PANEL)
    ]
    scale = [None] * tiles
    for j in range(PANEL):
        k, r = divmod(j, 8)
        s = lax.rsqrt(jnp.broadcast_to(bc[j][k][r : r + 1, :], (8, NB)))
        scale[k] = s if r == 0 else jnp.where(sub == r, s, scale[k])
        m = [(bc[j][q] * s) * s for q in range(tiles)]
        m[k] = jnp.where(sub > r, m[k], 0.0)

        def step(v):
            u = jnp.broadcast_to(v[k][r : r + 1, :], (8, NB))
            return [v[q] - m[q] * u if q >= k else v[q] for q in range(tiles)]

        for t in range(j + 1, PANEL):
            bc[t] = step(bc[t])
        rows = step(rows)
        inv = step(inv)
    inside = (lane >= base) & (lane < base + PANEL)
    new = [jnp.where(inside, inv[q], rows[q]) * scale[q] for q in range(tiles)]
    mult = [jnp.where(lane >= base + PANEL, new[q], 0.0) for q in range(tiles)]
    return new, mult


def block(x):
    n, tiles = NB // 8, PANEL // 8
    t = [x[8 * q : 8 * q + 8, :] for q in range(n)]
    lane = lax.broadcasted_iota(jnp.int32, (8, NB), 1)
    for p in range(NB // PANEL):
        lo, hi = tiles * p, tiles * (p + 1)
        new, mult = panel(t[lo:hi], p)
        t[lo:hi] = new
        if hi < n:
            upd = outer(jnp.concatenate(mult, 0), jnp.concatenate(new, 0))
            keep = (lane < PANEL * p) | (lane >= PANEL * (p + 1))
            for q in range(hi, n):
                t[q] = jnp.where(keep, t[q], 0.0) - upd[8 * q : 8 * q + 8, :]
    r = lax.broadcasted_iota(jnp.int32, (NB, NB), 0)
    c = lax.broadcasted_iota(jnp.int32, (NB, NB), 1)
    return jnp.where(r >= c, jnp.concatenate(t, 0), 0.0)


def inverse_kernel(n, k, g_ref, o_ref):
    a, b = k * NB, (k + 1) * NB
    x = block(g_ref[a:b, a:b])
    row = jnp.dot(x, g_ref[a:b, :], precision=HIGHEST, preferred_element_type=jnp.float32)
    lane = lax.broadcasted_iota(jnp.int32, (NB, n), 1)
    row = jnp.where((lane >= a) & (lane < b), jnp.concatenate([x] * (n // NB), 1), row)
    if k > 0:
        o_ref[:a, :] = g_ref[:a, :]
    o_ref[a:b, :] = jnp.where(lane < b, row, 0.0)
    if b < n:
        upd = lax.dot_general(
            row[:, b:],
            row,
            (((0,), (0,)), ((), ())),
            precision=HIGHEST,
            preferred_element_type=jnp.float32,
        )
        lane = lax.broadcasted_iota(jnp.int32, (n - b, n), 1)
        cur = jnp.where((lane >= a) & (lane < b), 0.0, g_ref[b:, :])
        o_ref[b:, :] = cur - upd


def inverse_step(g, k):
    n = g.shape[0]
    return pl.pallas_call(
        functools.partial(inverse_kernel, n, k),
        out_shape=jax.ShapeDtypeStruct((n, n), jnp.float32),
        in_specs=[pl.BlockSpec(memory_space=pltpu.VMEM)],
        out_specs=pl.BlockSpec(memory_space=pltpu.VMEM),
        compiler_params=pltpu.CompilerParams(vmem_limit_bytes=32 * 1024 * 1024),
        cost_estimate=pl.CostEstimate(
            flops=16 * 10**9, bytes_accessed=2 * n * n * 4, transcendentals=n
        ),
        name="inverse_step",
    )(g)


def pack(piece):
    rows, width = piece.shape
    whole = width // 128
    rest = piece[:, whole * 128 :]
    quarter = rows // 4
    side = [rest[q * quarter : (q + 1) * quarter] for q in range(4)]
    side.append(jnp.zeros((quarter, 128 - 4 * (width % 128)), piece.dtype))
    tiles = [piece[:, t * 128 : (t + 1) * 128] for t in range(whole)]
    return jnp.concatenate(tiles + [jnp.concatenate(side, 1)], 0)


def unpack(packed, rows, width):
    whole, left, quarter = width // 128, width % 128, rows // 4
    tiles = [packed[t * rows : (t + 1) * rows] for t in range(whole)]
    side = packed[whole * rows :]
    tiles.append(jnp.concatenate([side[:, q * left : (q + 1) * left] for q in range(4)], 0))
    return jnp.concatenate(tiles, 1)


def packed_rows(rows, width):
    return rows * (width // 128) + rows // 4


def cut_kernel(width, x_ref, o_ref):
    for j in range(o_ref.shape[0]):
        o_ref[j] = pack(x_ref[:, j * width : (j + 1) * width])


def cut_columns(x, parts):
    rows, width = x.shape[0], x.shape[1] // parts
    shape = (parts, packed_rows(rows, width), 128)
    return pl.pallas_call(
        functools.partial(cut_kernel, width),
        in_specs=[pl.BlockSpec(memory_space=pltpu.VMEM)],
        out_specs=pl.BlockSpec(memory_space=pltpu.VMEM),
        out_shape=jax.ShapeDtypeStruct(shape, x.dtype),
        compiler_params=pltpu.CompilerParams(vmem_limit_bytes=32 * 1024 * 1024),
        cost_estimate=pl.CostEstimate(
            flops=0, bytes_accessed=4 * rows * parts * width, transcendentals=0
        ),
        name="cut_columns",
    )(x)


def join_kernel(width, x_ref, o_ref):
    for j in range(x_ref.shape[0]):
        o_ref[:, j * width : (j + 1) * width] = unpack(x_ref[j], o_ref.shape[0], width)


def join_columns(x, rows, width):
    parts = x.shape[0]
    return pl.pallas_call(
        functools.partial(join_kernel, width),
        in_specs=[pl.BlockSpec(memory_space=pltpu.VMEM)],
        out_specs=pl.BlockSpec(memory_space=pltpu.VMEM),
        out_shape=jax.ShapeDtypeStruct((rows, parts * width), x.dtype),
        compiler_params=pltpu.CompilerParams(vmem_limit_bytes=32 * 1024 * 1024),
        cost_estimate=pl.CostEstimate(
            flops=0, bytes_accessed=4 * rows * parts * width, transcendentals=0
        ),
        name="join_columns",
    )(x)


def split2(x):
    hi = x.astype(jnp.bfloat16)
    return hi, (x - hi.astype(jnp.float32)).astype(jnp.bfloat16)


def dot3(a, b):
    f32 = jnp.float32
    return (
        jnp.dot(a[0], b[0], preferred_element_type=f32)
        + jnp.dot(a[0], b[1], preferred_element_type=f32)
        + jnp.dot(a[1], b[0], preferred_element_type=f32)
    )


def add_project_kernel(slot_ref, g_ref, m_ref, b_ref, s_ref, *refs):
    hi_ref, lo_ref = refs[8:]

    @pl.when(pl.program_id(0) == 0)
    def _():
        hi_ref[...], lo_ref[...] = split2(b_ref[...])

    rows, cols = m_ref.shape
    grad = [unpack(g_ref[k], rows // 4, cols) for k in range(4)]
    summed = m_ref[...] + jnp.concatenate(grad, 0).astype(jnp.float32)
    s_ref[...] = summed
    part = dot3(split2(summed), (hi_ref[...], lo_ref[...]))
    half = part.shape[1] // 2
    for side in range(2):
        slot = slot_ref[4 * side + pl.program_id(0)]
        for to in range(4):

            @pl.when(slot == to)
            def _(side=side, to=to):
                refs[4 * side + to][...] = part[:, side * half : (side + 1) * half]


def add_project(slots, grad, momentum, basis):
    rows, cols = momentum.shape
    rank = basis.shape[1]
    step = rows // 4
    return pl.pallas_call(
        add_project_kernel,
        grid=(rows // step,),
        in_specs=[
            pl.BlockSpec(memory_space=pltpu.SMEM),
            pl.BlockSpec((4,) + grad.shape[1:], lambda i: (i, 0, 0)),
            pl.BlockSpec((step, cols), lambda i: (i, 0)),
            pl.BlockSpec((cols, rank), lambda i: (0, 0)),
        ],
        out_specs=[
            pl.BlockSpec((step, cols), lambda i: (i, 0)),
        ]
        + [pl.BlockSpec((step, rank // 2), lambda i: (0, 0))] * 8,
        out_shape=[jax.ShapeDtypeStruct((rows, cols), jnp.float32)]
        + [jax.ShapeDtypeStruct((step, rank // 2), jnp.float32)] * 8,
        scratch_shapes=[pltpu.VMEM((cols, rank), jnp.bfloat16)] * 2,
        compiler_params=pltpu.CompilerParams(vmem_limit_bytes=36 * 1024 * 1024),
        cost_estimate=pl.CostEstimate(
            flops=6 * rows * cols * rank, bytes_accessed=10 * rows * cols, transcendentals=0
        ),
        name="add_project",
    )(slots, grad, momentum, basis)


def parts_kernel(x_ref, hi_ref, lo_ref):
    hi_ref[...], lo_ref[...] = split2(x_ref[...])


def parts_of(x):
    vmem = pl.BlockSpec(memory_space=pltpu.VMEM)
    return pl.pallas_call(
        parts_kernel,
        in_specs=[vmem],
        out_specs=[vmem, vmem],
        out_shape=[jax.ShapeDtypeStruct(x.shape, jnp.bfloat16)] * 2,
        compiler_params=pltpu.CompilerParams(vmem_limit_bytes=16 * 1024 * 1024),
        cost_estimate=pl.CostEstimate(
            flops=2 * x.size, bytes_accessed=8 * x.size, transcendentals=0
        ),
        name="parts",
    )(x)


def update_kernel(q_ref, scale_ref, hi_ref, lo_ref, o_ref):
    q = split2(q_ref[...] * scale_ref[...])
    dims = (((1,), (1,)), ((), ()))
    f32 = jnp.float32
    out = lax.dot_general(q[0], hi_ref[...], dims, preferred_element_type=f32)
    out += lax.dot_general(q[0], lo_ref[...], dims, preferred_element_type=f32)
    out += lax.dot_general(q[1], hi_ref[...], dims, preferred_element_type=f32)
    out = out.astype(jnp.bfloat16)
    part = out.shape[0] // 4
    for k in range(4):
        o_ref[k] = pack(out[k * part : (k + 1) * part])


def update_of(orthonormal, scale, parts):
    rows, rank = orthonormal.shape
    cols = parts[0].shape[0]
    step = rows // 4
    packed = packed_rows(rows // 16, cols)
    whole = pl.BlockSpec((cols, rank), lambda i: (0, 0))
    return pl.pallas_call(
        update_kernel,
        grid=(4,),
        in_specs=[
            pl.BlockSpec((step, rank), lambda i: (i, 0)),
            pl.BlockSpec((1, rank), lambda i: (0, 0)),
            whole,
            whole,
        ],
        out_specs=pl.BlockSpec((4, packed, 128), lambda i: (i, 0, 0)),
        out_shape=jax.ShapeDtypeStruct((16, packed, 128), jnp.bfloat16),
        compiler_params=pltpu.CompilerParams(vmem_limit_bytes=32 * 1024 * 1024),
        cost_estimate=pl.CostEstimate(
            flops=6 * rows * cols * rank, bytes_accessed=4 * rows * cols, transcendentals=0
        ),
        name="update_tile",
    )(orthonormal, scale, *parts)


def shift(x, axis, d, n=4):
    return lax.ppermute(x, axis, [(i, (i + d) % n) for i in range(n)])


def other_core(x):
    return lax.ppermute(x, "c", [(0, 1), (1, 0)])


def partners(axis):
    i = lax.axis_index(axis)
    first = lax.axis_index("c") == 0
    one, two = jnp.bitwise_xor(i, 1), 3 - i
    return i, jnp.where(first, one, two), jnp.where(first, two, one), jnp.bitwise_xor(i, 2)


def swap(x, axis, turn):
    perm = []
    for c in range(2):
        for i in range(4):
            j = i ^ 1 if c == turn else 3 - i
            perm.append((2 * i + c, 2 * j + c) if axis == "y" else (4 * c + i, 4 * c + j))
    return lax.ppermute(x, ("y", "c") if axis == "y" else ("c", axis), perm)


def pick(x, i):
    return lax.dynamic_index_in_dim(x, i, 0, False)


def slots_of(axis):
    i, p1, p2, far = partners(axis)
    k = jnp.arange(4, dtype=jnp.int32)
    return jnp.where(k == i, 0, jnp.where(k == p2, 1, jnp.where(k == p1, 2, 3))).astype(jnp.int32)


def pair_scatter_start(parts, axis):
    got_far = swap(parts[3], axis, 0)
    got_own = swap(parts[2], axis, 0)
    return parts[0], got_own, swap(parts[1] + got_far, axis, 1)


def pair_scatter(parts, axis):
    return sum_parts(pair_scatter_start(parts, axis))


def sum_parts(parts):
    return parts[0] + parts[1] + parts[2]


def quarters(x, axis):
    i, p1, p2, far = partners(axis)
    return [pick(x, k) for k in (i, p2, p1, far)]


def pair_gather_start(x, axis):
    return x, swap(x, axis, 1), swap(x, axis, 0)


def place(parts, axis):
    i, p1, p2, far = partners(axis)
    out = jnp.zeros((4,) + parts[0].shape, parts[0].dtype)
    for where, part in zip((i, p2, p1, far), parts):
        out = lax.dynamic_update_index_in_dim(out, part, where, 0)
    return out


def pair_gather(x, axis):
    parts = pair_gather_start(x, axis)
    return place((*parts, swap(parts[1], axis, 0)), axis)


def pair_sum(x, axis):
    x = x + swap(x, axis, 0)
    return x + swap(x, axis, 1)


def direct_gather(x, axis):
    me = lax.axis_index(axis)
    out = jnp.zeros((4,) + x.shape, x.dtype)
    for d, part in ((0, x), (3, shift(x, axis, 1)), (2, shift(x, axis, 2)), (1, shift(x, axis, 3))):
        out = lax.dynamic_update_index_in_dim(out, part, (me + d) % 4, 0)
    return out


def direct_sum(x, axis):
    return (x + shift(x, axis, 2)) + (shift(x, axis, 1) + shift(x, axis, 3))


def reduce_projected(left, right):
    a, b = pair_scatter(left, "z"), pair_scatter(right, "x")
    a, b = pair_sum(a, "x"), pair_sum(b, "z")
    a, b = pair_gather(a, "z"), pair_gather(b, "x")
    rows, w = 4 * a.shape[1], a.shape[2]
    return jnp.concatenate([a.reshape(rows, w), b.reshape(rows, w)], 1)


def both_halves(mine):
    first = lax.axis_index("c") == 0
    theirs = other_core(mine)
    return jnp.concatenate([jnp.where(first, mine, theirs), jnp.where(first, theirs, mine)], 1)


def core_scatter(x):
    first = lax.axis_index("c") == 0
    left, right = jnp.split(x, 2, axis=1)
    return jnp.where(first, left, right) + other_core(jnp.where(first, right, left))


def gram_slab(projected):
    slab = projected.shape[1] // 4
    mine = lax.dynamic_slice_in_dim(projected, lax.axis_index("z") * slab, slab, 1)
    return lax.dot_general(mine, projected, (((0,), (0,)), ((), ())), precision=HIGHEST)


def gram_gather(part):
    n = 4 * part.shape[0]
    return both_halves(direct_gather(part, "z").reshape(n, n // 2))


def local(gradient, momentum, basis):
    rows, cols = momentum.shape
    pieces = lax.all_to_all(cut_columns(gradient, 16), ("z", "x"), 0, 0, tiled=True)
    slots = jnp.concatenate([slots_of("z"), slots_of("x")])
    summed, *partial = add_project(slots, pieces, momentum, basis)
    projected = reduce_projected(partial[:4], partial[4:])
    slab = gram_slab(projected)
    dims = (((0,), (0,)), ((), ()))
    half = RANK // 2
    stages = (
        (core_scatter, lambda p: lax.dot_general(summed, p, dims, precision=HIGH)),
        (
            lambda g: direct_sum(g, "y"),
            lambda w: core_scatter(jnp.pad(w, ((0, -cols % 32), (0, 0)))),
        ),
        (gram_gather, lambda w: pair_scatter(quarters(w.reshape(4, -1, half), "y"), "y")),
        (lambda g: inverse_step(g, 0), lambda w: pair_gather_start(w, "y")),
        (lambda g: inverse_step(g, 1), lambda w: (*w, swap(w[1], "y", 0))),
        (lambda g: inverse_step(g, 2), lambda w: place(w, "y")),
        (lambda g: inverse_step(g, 3), lambda w: both_halves(w.reshape(-1, half))),
    )
    mixed = projected
    inverse = slab
    for of_gram, of_mixed in stages:
        inverse, mixed = lax.optimization_barrier((inverse, mixed))
        inverse, mixed = of_gram(inverse), of_mixed(mixed)
    mixed = mixed[:cols]
    contract = (((1,), (1,)), ((), ()))
    orthonormal = lax.dot_general(projected, inverse, contract, precision=HIGH)
    right_factor = lax.dot_general(mixed, inverse, contract, precision=HIGH)
    squares = jnp.sum(right_factor * right_factor, axis=0, keepdims=True)
    squares = direct_sum(jnp.broadcast_to(squares, (8, RANK)), "z")
    parts = parts_of(right_factor)
    squares = direct_sum(squares, "x")[:1]
    inverse_norm = lax.rsqrt(squares + epsilon)
    scaling = (D * FF / RANK) ** 0.5
    update_tile = update_of(orthonormal, scaling * inverse_norm, parts)
    pieces = lax.all_to_all(update_tile, ("z", "x"), 0, 0, tiled=True)
    right_factor, _ = lax.optimization_barrier((right_factor, update_tile))
    new_basis = right_factor * inverse_norm
    new_momentum = summed - feedback_keep * lax.dot_general(
        orthonormal, right_factor, contract, precision=HIGH
    )
    return (join_columns(pieces, rows // 16, cols), new_momentum, new_basis)


def solution(mesh):
    fine = Mesh(mesh.devices.reshape(4, 2, 4, 4), ("y", "c", "z", "x"))
    row, col = ("y", "c"), ("z", "x")
    return jax.shard_map(
        local,
        mesh=fine,
        in_specs=(P(row + col, None), P(row, col), P(col, None)),
        out_specs=(P(row + col, None), P(row, col), P(col, None)),
        check_vma=False,
    )
```

```python
import functools

import jax
import jax.numpy as jnp
from jax import lax
from jax.experimental import pallas as pl
from jax.experimental.pallas import tpu as pltpu
from jax.sharding import Mesh, PartitionSpec as P

D = 8192
FF = 14784
RANK = 512
NB = 128
PANEL = 16

feedback_keep = 0.05
epsilon = 1e-06

HIGHEST = lax.Precision.HIGHEST
HIGH = lax.Precision.HIGH


def split3(x):
    a = x.astype(jnp.bfloat16)
    r = x - a.astype(jnp.float32)
    b = r.astype(jnp.bfloat16)
    c = (r - b.astype(jnp.float32)).astype(jnp.bfloat16)
    return [t.astype(jnp.float32) for t in (a, b, c)]


def outer(u, v):
    a1, a2, a3 = split3(u)
    b1, b2, b3 = split3(v)
    ul = jnp.concatenate([a1, a1, a2, a2, a1, a3], 0).astype(jnp.bfloat16)
    vl = jnp.concatenate([b1, b2, b1, b2, b3, b1], 0).astype(jnp.bfloat16)
    return lax.dot_general(
        ul, vl, (((0,), (0,)), ((), ())), preferred_element_type=jnp.float32
    )


def panel(rows, p):
    base = PANEL * p
    tiles = PANEL // 8
    lane = lax.broadcasted_iota(jnp.int32, (8, NB), 1)
    sub = lax.broadcasted_iota(jnp.int32, (8, NB), 0)
    inv = [jnp.where(lane == sub + base + 8 * q, 1.0, 0.0).astype(jnp.float32) for q in range(tiles)]
    bc = [
        [jnp.broadcast_to(rows[q][:, base + t : base + t + 1], (8, NB)) for q in range(tiles)]
        for t in range(PANEL)
    ]
    scale = [None] * tiles
    for j in range(PANEL):
        k, r = divmod(j, 8)
        s = lax.rsqrt(jnp.broadcast_to(bc[j][k][r : r + 1, :], (8, NB)))
        scale[k] = s if r == 0 else jnp.where(sub == r, s, scale[k])
        m = [(bc[j][q] * s) * s for q in range(tiles)]
        m[k] = jnp.where(sub > r, m[k], 0.0)

        def step(v):
            u = jnp.broadcast_to(v[k][r : r + 1, :], (8, NB))
            return [v[q] - m[q] * u if q >= k else v[q] for q in range(tiles)]

        for t in range(j + 1, PANEL):
            bc[t] = step(bc[t])
        rows = step(rows)
        inv = step(inv)
    inside = (lane >= base) & (lane < base + PANEL)
    new = [jnp.where(inside, inv[q], rows[q]) * scale[q] for q in range(tiles)]
    mult = [jnp.where(lane >= base + PANEL, new[q], 0.0) for q in range(tiles)]
    return new, mult


def block(x):
    n, tiles = NB // 8, PANEL // 8
    t = [x[8 * q : 8 * q + 8, :] for q in range(n)]
    lane = lax.broadcasted_iota(jnp.int32, (8, NB), 1)
    for p in range(NB // PANEL):
        lo, hi = tiles * p, tiles * (p + 1)
        new, mult = panel(t[lo:hi], p)
        t[lo:hi] = new
        if hi < n:
            upd = outer(jnp.concatenate(mult, 0), jnp.concatenate(new, 0))
            keep = (lane < PANEL * p) | (lane >= PANEL * (p + 1))
            for q in range(hi, n):
                t[q] = jnp.where(keep, t[q], 0.0) - upd[8 * q : 8 * q + 8, :]
    r = lax.broadcasted_iota(jnp.int32, (NB, NB), 0)
    c = lax.broadcasted_iota(jnp.int32, (NB, NB), 1)
    return jnp.where(r >= c, jnp.concatenate(t, 0), 0.0)


def inverse_kernel(n, k, g_ref, o_ref):
    a, b = k * NB, (k + 1) * NB
    x = block(g_ref[a:b, a:b])
    row = jnp.dot(x, g_ref[a:b, :], precision=HIGHEST, preferred_element_type=jnp.float32)
    lane = lax.broadcasted_iota(jnp.int32, (NB, n), 1)
    row = jnp.where((lane >= a) & (lane < b), jnp.concatenate([x] * (n // NB), 1), row)
    if k > 0:
        o_ref[:a, :] = g_ref[:a, :]
    o_ref[a:b, :] = jnp.where(lane < b, row, 0.0)
    if b < n:
        upd = lax.dot_general(
            row[:, b:],
            row,
            (((0,), (0,)), ((), ())),
            precision=HIGHEST,
            preferred_element_type=jnp.float32,
        )
        lane = lax.broadcasted_iota(jnp.int32, (n - b, n), 1)
        cur = jnp.where((lane >= a) & (lane < b), 0.0, g_ref[b:, :])
        o_ref[b:, :] = cur - upd


def inverse_step(g, k):
    n = g.shape[0]
    return pl.pallas_call(
        functools.partial(inverse_kernel, n, k),
        out_shape=jax.ShapeDtypeStruct((n, n), jnp.float32),
        in_specs=[pl.BlockSpec(memory_space=pltpu.VMEM)],
        out_specs=pl.BlockSpec(memory_space=pltpu.VMEM),
        compiler_params=pltpu.CompilerParams(vmem_limit_bytes=32 * 1024 * 1024),
        cost_estimate=pl.CostEstimate(
            flops=16 * 10**9, bytes_accessed=2 * n * n * 4, transcendentals=n
        ),
        name="inverse_step",
    )(g)


def pack(piece):
    rows, width = piece.shape
    whole = width // 128
    rest = piece[:, whole * 128 :]
    quarter = rows // 4
    side = [rest[q * quarter : (q + 1) * quarter] for q in range(4)]
    side.append(jnp.zeros((quarter, 128 - 4 * (width % 128)), piece.dtype))
    tiles = [piece[:, t * 128 : (t + 1) * 128] for t in range(whole)]
    return jnp.concatenate(tiles + [jnp.concatenate(side, 1)], 0)


def unpack(packed, rows, width):
    whole, left, quarter = width // 128, width % 128, rows // 4
    tiles = [packed[t * rows : (t + 1) * rows] for t in range(whole)]
    side = packed[whole * rows :]
    tiles.append(jnp.concatenate([side[:, q * left : (q + 1) * left] for q in range(4)], 0))
    return jnp.concatenate(tiles, 1)


def packed_rows(rows, width):
    return rows * (width // 128) + rows // 4


def cut_kernel(width, x_ref, o_ref):
    for j in range(o_ref.shape[0]):
        o_ref[j] = pack(x_ref[:, j * width : (j + 1) * width])


def cut_columns(x, parts):
    rows, width = x.shape[0], x.shape[1] // parts
    shape = (parts, packed_rows(rows, width), 128)
    return pl.pallas_call(
        functools.partial(cut_kernel, width),
        in_specs=[pl.BlockSpec(memory_space=pltpu.VMEM)],
        out_specs=pl.BlockSpec(memory_space=pltpu.VMEM),
        out_shape=jax.ShapeDtypeStruct(shape, x.dtype),
        compiler_params=pltpu.CompilerParams(vmem_limit_bytes=32 * 1024 * 1024),
        cost_estimate=pl.CostEstimate(
            flops=0, bytes_accessed=4 * rows * parts * width, transcendentals=0
        ),
        name="cut_columns",
    )(x)


def join_kernel(width, x_ref, o_ref):
    for j in range(x_ref.shape[0]):
        o_ref[:, j * width : (j + 1) * width] = unpack(x_ref[j], o_ref.shape[0], width)


def join_columns(x, rows, width):
    parts = x.shape[0]
    return pl.pallas_call(
        functools.partial(join_kernel, width),
        in_specs=[pl.BlockSpec(memory_space=pltpu.VMEM)],
        out_specs=pl.BlockSpec(memory_space=pltpu.VMEM),
        out_shape=jax.ShapeDtypeStruct((rows, parts * width), x.dtype),
        compiler_params=pltpu.CompilerParams(vmem_limit_bytes=32 * 1024 * 1024),
        cost_estimate=pl.CostEstimate(
            flops=0, bytes_accessed=4 * rows * parts * width, transcendentals=0
        ),
        name="join_columns",
    )(x)


def split2(x):
    hi = x.astype(jnp.bfloat16)
    return hi, (x - hi.astype(jnp.float32)).astype(jnp.bfloat16)


def dot3(a, b):
    f32 = jnp.float32
    return (
        jnp.dot(a[0], b[0], preferred_element_type=f32)
        + jnp.dot(a[0], b[1], preferred_element_type=f32)
        + jnp.dot(a[1], b[0], preferred_element_type=f32)
    )


def add_project_kernel(slot_ref, g_ref, m_ref, b_ref, s_ref, *refs):
    hi_ref, lo_ref = refs[8:]

    @pl.when(pl.program_id(0) == 0)
    def _():
        hi_ref[...], lo_ref[...] = split2(b_ref[...])

    rows, cols = m_ref.shape
    grad = [unpack(g_ref[k], rows // 4, cols) for k in range(4)]
    summed = m_ref[...] + jnp.concatenate(grad, 0).astype(jnp.float32)
    s_ref[...] = summed
    part = dot3(split2(summed), (hi_ref[...], lo_ref[...]))
    half = part.shape[1] // 2
    for side in range(2):
        slot = slot_ref[4 * side + pl.program_id(0)]
        for to in range(4):

            @pl.when(slot == to)
            def _(side=side, to=to):
                refs[4 * side + to][...] = part[:, side * half : (side + 1) * half]


def add_project(slots, grad, momentum, basis):
    rows, cols = momentum.shape
    rank = basis.shape[1]
    step = rows // 4
    return pl.pallas_call(
        add_project_kernel,
        grid=(rows // step,),
        in_specs=[
            pl.BlockSpec(memory_space=pltpu.SMEM),
            pl.BlockSpec((4,) + grad.shape[1:], lambda i: (i, 0, 0)),
            pl.BlockSpec((step, cols), lambda i: (i, 0)),
            pl.BlockSpec((cols, rank), lambda i: (0, 0)),
        ],
        out_specs=[
            pl.BlockSpec((step, cols), lambda i: (i, 0)),
        ]
        + [pl.BlockSpec((step, rank // 2), lambda i: (0, 0))] * 8,
        out_shape=[jax.ShapeDtypeStruct((rows, cols), jnp.float32)]
        + [jax.ShapeDtypeStruct((step, rank // 2), jnp.float32)] * 8,
        scratch_shapes=[pltpu.VMEM((cols, rank), jnp.bfloat16)] * 2,
        compiler_params=pltpu.CompilerParams(vmem_limit_bytes=36 * 1024 * 1024),
        cost_estimate=pl.CostEstimate(
            flops=6 * rows * cols * rank, bytes_accessed=10 * rows * cols, transcendentals=0
        ),
        name="add_project",
    )(slots, grad, momentum, basis)


def parts_kernel(x_ref, hi_ref, lo_ref):
    hi_ref[...], lo_ref[...] = split2(x_ref[...])


def parts_of(x):
    vmem = pl.BlockSpec(memory_space=pltpu.VMEM)
    return pl.pallas_call(
        parts_kernel,
        in_specs=[vmem],
        out_specs=[vmem, vmem],
        out_shape=[jax.ShapeDtypeStruct(x.shape, jnp.bfloat16)] * 2,
        compiler_params=pltpu.CompilerParams(vmem_limit_bytes=16 * 1024 * 1024),
        cost_estimate=pl.CostEstimate(
            flops=2 * x.size, bytes_accessed=8 * x.size, transcendentals=0
        ),
        name="parts",
    )(x)


def update_kernel(q_ref, scale_ref, hi_ref, lo_ref, o_ref):
    q = split2(q_ref[...] * scale_ref[...])
    dims = (((1,), (1,)), ((), ()))
    f32 = jnp.float32
    out = lax.dot_general(q[0], hi_ref[...], dims, preferred_element_type=f32)
    out += lax.dot_general(q[0], lo_ref[...], dims, preferred_element_type=f32)
    out += lax.dot_general(q[1], hi_ref[...], dims, preferred_element_type=f32)
    out = out.astype(jnp.bfloat16)
    part = out.shape[0] // 4
    for k in range(4):
        o_ref[k] = pack(out[k * part : (k + 1) * part])


def update_of(orthonormal, scale, parts):
    rows, rank = orthonormal.shape
    cols = parts[0].shape[0]
    step = rows // 4
    packed = packed_rows(rows // 16, cols)
    whole = pl.BlockSpec((cols, rank), lambda i: (0, 0))
    return pl.pallas_call(
        update_kernel,
        grid=(4,),
        in_specs=[
            pl.BlockSpec((step, rank), lambda i: (i, 0)),
            pl.BlockSpec((1, rank), lambda i: (0, 0)),
            whole,
            whole,
        ],
        out_specs=pl.BlockSpec((4, packed, 128), lambda i: (i, 0, 0)),
        out_shape=jax.ShapeDtypeStruct((16, packed, 128), jnp.bfloat16),
        compiler_params=pltpu.CompilerParams(vmem_limit_bytes=32 * 1024 * 1024),
        cost_estimate=pl.CostEstimate(
            flops=6 * rows * cols * rank, bytes_accessed=4 * rows * cols, transcendentals=0
        ),
        name="update_tile",
    )(orthonormal, scale, *parts)


def other_core(x):
    return lax.ppermute(x, "c", [(0, 1), (1, 0)])


def partners(axis):
    i = lax.axis_index(axis)
    first = lax.axis_index("c") == 0
    one, two = jnp.bitwise_xor(i, 1), 3 - i
    return i, jnp.where(first, one, two), jnp.where(first, two, one), jnp.bitwise_xor(i, 2)


def swap(x, axis, turn):
    perm = []
    for c in range(2):
        for i in range(4):
            j = i ^ 1 if c == turn else 3 - i
            perm.append((2 * i + c, 2 * j + c) if axis == "y" else (4 * c + i, 4 * c + j))
    return lax.ppermute(x, ("y", "c") if axis == "y" else ("c", axis), perm)


def pick(x, i):
    return lax.dynamic_index_in_dim(x, i, 0, False)


def slots_of(axis):
    i, p1, p2, far = partners(axis)
    k = jnp.arange(4, dtype=jnp.int32)
    return jnp.where(k == i, 0, jnp.where(k == p2, 1, jnp.where(k == p1, 2, 3))).astype(jnp.int32)


def pair_scatter_start(parts, axis):
    got_far = swap(parts[3], axis, 0)
    got_own = swap(parts[2], axis, 0)
    return parts[0], got_own, swap(parts[1] + got_far, axis, 1)


def pair_scatter(parts, axis):
    return sum_parts(pair_scatter_start(parts, axis))


def sum_parts(parts):
    return parts[0] + parts[1] + parts[2]


def quarters(x, axis):
    i, p1, p2, far = partners(axis)
    return [pick(x, k) for k in (i, p2, p1, far)]


def pair_gather_start(x, axis):
    return x, swap(x, axis, 1), swap(x, axis, 0)


def place(parts, axis):
    i, p1, p2, far = partners(axis)
    out = jnp.zeros((4,) + parts[0].shape, parts[0].dtype)
    for where, part in zip((i, p2, p1, far), parts):
        out = lax.dynamic_update_index_in_dim(out, part, where, 0)
    return out


def pair_gather(x, axis):
    parts = pair_gather_start(x, axis)
    return place((*parts, swap(parts[1], axis, 0)), axis)


def pair_sum(x, axis):
    x = x + swap(x, axis, 0)
    return x + swap(x, axis, 1)


def flip(x, axis, d):
    return lax.ppermute(x, axis, [(i, i ^ d) for i in range(4)])


def direct_gather(x, axis):
    me = lax.axis_index(axis)
    out = jnp.zeros((4,) + x.shape, x.dtype)
    for d, part in enumerate((x, flip(x, axis, 1), flip(x, axis, 2), flip(x, axis, 3))):
        out = lax.dynamic_update_index_in_dim(out, part, jnp.bitwise_xor(me, d), 0)
    return out


def direct_sum(x, axis):
    return (x + flip(x, axis, 2)) + (flip(x, axis, 1) + flip(x, axis, 3))


def reduce_projected(left, right):
    a, b = pair_scatter(left, "z"), pair_scatter(right, "x")
    a, b = pair_sum(a, "x"), pair_sum(b, "z")
    a, b = pair_gather(a, "z"), pair_gather(b, "x")
    rows, w = 4 * a.shape[1], a.shape[2]
    return jnp.concatenate([a.reshape(rows, w), b.reshape(rows, w)], 1)


def both_halves(mine):
    first = lax.axis_index("c") == 0
    theirs = other_core(mine)
    return jnp.concatenate([jnp.where(first, mine, theirs), jnp.where(first, theirs, mine)], 1)


def core_scatter(x):
    first = lax.axis_index("c") == 0
    left, right = jnp.split(x, 2, axis=1)
    return jnp.where(first, left, right) + other_core(jnp.where(first, right, left))


def gram_slab(projected):
    slab = projected.shape[1] // 4
    mine = lax.dynamic_slice_in_dim(projected, lax.axis_index("z") * slab, slab, 1)
    return lax.dot_general(mine, projected, (((0,), (0,)), ((), ())), precision=HIGHEST)


def gram_gather(part):
    n = 4 * part.shape[0]
    return both_halves(direct_gather(part, "z").reshape(n, n // 2))


def local(gradient, momentum, basis):
    rows, cols = momentum.shape
    pieces = lax.all_to_all(cut_columns(gradient, 16), ("z", "x"), 0, 0, tiled=True)
    slots = jnp.concatenate([slots_of("z"), slots_of("x")])
    summed, *partial = add_project(slots, pieces, momentum, basis)
    projected = reduce_projected(partial[:4], partial[4:])
    slab = gram_slab(projected)
    dims = (((0,), (0,)), ((), ()))
    half = RANK // 2
    stages = (
        (core_scatter, lambda p: lax.dot_general(summed, p, dims, precision=HIGH)),
        (
            lambda g: direct_sum(g, "y"),
            lambda w: core_scatter(jnp.pad(w, ((0, -cols % 32), (0, 0)))),
        ),
        (gram_gather, lambda w: pair_scatter(quarters(w.reshape(4, -1, half), "y"), "y")),
        (lambda g: inverse_step(g, 0), lambda w: pair_gather_start(w, "y")),
        (lambda g: inverse_step(g, 1), lambda w: (*w, swap(w[1], "y", 0))),
        (lambda g: inverse_step(g, 2), lambda w: place(w, "y")),
        (lambda g: inverse_step(g, 3), lambda w: both_halves(w.reshape(-1, half))),
    )
    mixed = projected
    inverse = slab
    for of_gram, of_mixed in stages:
        inverse, mixed = lax.optimization_barrier((inverse, mixed))
        inverse, mixed = of_gram(inverse), of_mixed(mixed)
    mixed = mixed[:cols]
    contract = (((1,), (1,)), ((), ()))
    orthonormal = lax.dot_general(projected, inverse, contract, precision=HIGH)
    right_factor = lax.dot_general(mixed, inverse, contract, precision=HIGH)
    squares = jnp.sum(right_factor * right_factor, axis=0, keepdims=True)
    squares = direct_sum(jnp.broadcast_to(squares, (8, RANK)), "z")
    parts = parts_of(right_factor)
    squares = direct_sum(squares, "x")[:1]
    inverse_norm = lax.rsqrt(squares + epsilon)
    scaling = (D * FF / RANK) ** 0.5
    update_tile = update_of(orthonormal, scaling * inverse_norm, parts)
    pieces = lax.all_to_all(update_tile, ("z", "x"), 0, 0, tiled=True)
    right_factor, _ = lax.optimization_barrier((right_factor, update_tile))
    new_basis = right_factor * inverse_norm
    new_momentum = summed - feedback_keep * lax.dot_general(
        orthonormal, right_factor, contract, precision=HIGH
    )
    return (join_columns(pieces, rows // 16, cols), new_momentum, new_basis)


def solution(mesh):
    fine = Mesh(mesh.devices.reshape(4, 2, 4, 4), ("y", "c", "z", "x"))
    row, col = ("y", "c"), ("z", "x")
    return jax.shard_map(
        local,
        mesh=fine,
        in_specs=(P(row + col, None), P(row, col), P(col, None)),
        out_specs=(P(row + col, None), P(row, col), P(col, None)),
        check_vma=False,
    )
```

```python
import functools

import jax
import jax.numpy as jnp
from jax import lax
from jax.experimental import pallas as pl
from jax.experimental.pallas import tpu as pltpu
from jax.sharding import Mesh, PartitionSpec as P

D = 8192
FF = 14784
RANK = 512
NB = 128
PANEL = 16

feedback_keep = 0.05
epsilon = 1e-06

HIGHEST = lax.Precision.HIGHEST
HIGH = lax.Precision.HIGH


def split3(x):
    a = x.astype(jnp.bfloat16)
    r = x - a.astype(jnp.float32)
    b = r.astype(jnp.bfloat16)
    c = (r - b.astype(jnp.float32)).astype(jnp.bfloat16)
    return [t.astype(jnp.float32) for t in (a, b, c)]


def outer(u, v):
    a1, a2, a3 = split3(u)
    b1, b2, b3 = split3(v)
    ul = jnp.concatenate([a1, a1, a2, a2, a1, a3], 0).astype(jnp.bfloat16)
    vl = jnp.concatenate([b1, b2, b1, b2, b3, b1], 0).astype(jnp.bfloat16)
    return lax.dot_general(
        ul, vl, (((0,), (0,)), ((), ())), preferred_element_type=jnp.float32
    )


def panel(rows, p):
    base = PANEL * p
    tiles = PANEL // 8
    lane = lax.broadcasted_iota(jnp.int32, (8, NB), 1)
    sub = lax.broadcasted_iota(jnp.int32, (8, NB), 0)
    inv = [jnp.where(lane == sub + base + 8 * q, 1.0, 0.0).astype(jnp.float32) for q in range(tiles)]
    bc = [
        [jnp.broadcast_to(rows[q][:, base + t : base + t + 1], (8, NB)) for q in range(tiles)]
        for t in range(PANEL)
    ]
    scale = [None] * tiles
    for j in range(PANEL):
        k, r = divmod(j, 8)
        s = lax.rsqrt(jnp.broadcast_to(bc[j][k][r : r + 1, :], (8, NB)))
        scale[k] = s if r == 0 else jnp.where(sub == r, s, scale[k])
        m = [(bc[j][q] * s) * s for q in range(tiles)]
        m[k] = jnp.where(sub > r, m[k], 0.0)

        def step(v):
            u = jnp.broadcast_to(v[k][r : r + 1, :], (8, NB))
            return [v[q] - m[q] * u if q >= k else v[q] for q in range(tiles)]

        for t in range(j + 1, PANEL):
            bc[t] = step(bc[t])
        rows = step(rows)
        inv = step(inv)
    inside = (lane >= base) & (lane < base + PANEL)
    new = [jnp.where(inside, inv[q], rows[q]) * scale[q] for q in range(tiles)]
    mult = [jnp.where(lane >= base + PANEL, new[q], 0.0) for q in range(tiles)]
    return new, mult


def block(x):
    n, tiles = NB // 8, PANEL // 8
    t = [x[8 * q : 8 * q + 8, :] for q in range(n)]
    lane = lax.broadcasted_iota(jnp.int32, (8, NB), 1)
    for p in range(NB // PANEL):
        lo, hi = tiles * p, tiles * (p + 1)
        new, mult = panel(t[lo:hi], p)
        t[lo:hi] = new
        if hi < n:
            upd = outer(jnp.concatenate(mult, 0), jnp.concatenate(new, 0))
            keep = (lane < PANEL * p) | (lane >= PANEL * (p + 1))
            for q in range(hi, n):
                t[q] = jnp.where(keep, t[q], 0.0) - upd[8 * q : 8 * q + 8, :]
    r = lax.broadcasted_iota(jnp.int32, (NB, NB), 0)
    c = lax.broadcasted_iota(jnp.int32, (NB, NB), 1)
    return jnp.where(r >= c, jnp.concatenate(t, 0), 0.0)


def inverse_kernel(n, k, g_ref, o_ref):
    a, b = k * NB, (k + 1) * NB
    x = block(g_ref[a:b, a:b])
    row = jnp.dot(x, g_ref[a:b, :], precision=HIGHEST, preferred_element_type=jnp.float32)
    lane = lax.broadcasted_iota(jnp.int32, (NB, n), 1)
    row = jnp.where((lane >= a) & (lane < b), jnp.concatenate([x] * (n // NB), 1), row)
    if k > 0:
        o_ref[:a, :] = g_ref[:a, :]
    o_ref[a:b, :] = jnp.where(lane < b, row, 0.0)
    if b < n:
        upd = lax.dot_general(
            row[:, b:],
            row,
            (((0,), (0,)), ((), ())),
            precision=HIGHEST,
            preferred_element_type=jnp.float32,
        )
        lane = lax.broadcasted_iota(jnp.int32, (n - b, n), 1)
        cur = jnp.where((lane >= a) & (lane < b), 0.0, g_ref[b:, :])
        o_ref[b:, :] = cur - upd


def inverse_step(g, k):
    n = g.shape[0]
    return pl.pallas_call(
        functools.partial(inverse_kernel, n, k),
        out_shape=jax.ShapeDtypeStruct((n, n), jnp.float32),
        in_specs=[pl.BlockSpec(memory_space=pltpu.VMEM)],
        out_specs=pl.BlockSpec(memory_space=pltpu.VMEM),
        compiler_params=pltpu.CompilerParams(vmem_limit_bytes=32 * 1024 * 1024),
        cost_estimate=pl.CostEstimate(
            flops=16 * 10**9, bytes_accessed=2 * n * n * 4, transcendentals=n
        ),
        name="inverse_step",
    )(g)


def pack(piece):
    rows, width = piece.shape
    whole = width // 128
    rest = piece[:, whole * 128 :]
    quarter = rows // 4
    side = [rest[q * quarter : (q + 1) * quarter] for q in range(4)]
    side.append(jnp.zeros((quarter, 128 - 4 * (width % 128)), piece.dtype))
    tiles = [piece[:, t * 128 : (t + 1) * 128] for t in range(whole)]
    return jnp.concatenate(tiles + [jnp.concatenate(side, 1)], 0)


def unpack(packed, rows, width):
    whole, left, quarter = width // 128, width % 128, rows // 4
    tiles = [packed[t * rows : (t + 1) * rows] for t in range(whole)]
    side = packed[whole * rows :]
    tiles.append(jnp.concatenate([side[:, q * left : (q + 1) * left] for q in range(4)], 0))
    return jnp.concatenate(tiles, 1)


def packed_rows(rows, width):
    return rows * (width // 128) + rows // 4


def cut_kernel(width, x_ref, o_ref):
    for j in range(o_ref.shape[0]):
        o_ref[j] = pack(x_ref[:, j * width : (j + 1) * width])


def cut_columns(x, parts):
    rows, width = x.shape[0], x.shape[1] // parts
    shape = (parts, packed_rows(rows, width), 128)
    return pl.pallas_call(
        functools.partial(cut_kernel, width),
        in_specs=[pl.BlockSpec(memory_space=pltpu.VMEM)],
        out_specs=pl.BlockSpec(memory_space=pltpu.VMEM),
        out_shape=jax.ShapeDtypeStruct(shape, x.dtype),
        compiler_params=pltpu.CompilerParams(vmem_limit_bytes=32 * 1024 * 1024),
        cost_estimate=pl.CostEstimate(
            flops=0, bytes_accessed=4 * rows * parts * width, transcendentals=0
        ),
        name="cut_columns",
    )(x)


def join_kernel(width, x_ref, o_ref):
    for j in range(x_ref.shape[0]):
        o_ref[:, j * width : (j + 1) * width] = unpack(x_ref[j], o_ref.shape[0], width)


def join_columns(x, rows, width):
    parts = x.shape[0]
    return pl.pallas_call(
        functools.partial(join_kernel, width),
        in_specs=[pl.BlockSpec(memory_space=pltpu.VMEM)],
        out_specs=pl.BlockSpec(memory_space=pltpu.VMEM),
        out_shape=jax.ShapeDtypeStruct((rows, parts * width), x.dtype),
        compiler_params=pltpu.CompilerParams(vmem_limit_bytes=32 * 1024 * 1024),
        cost_estimate=pl.CostEstimate(
            flops=0, bytes_accessed=4 * rows * parts * width, transcendentals=0
        ),
        name="join_columns",
    )(x)


def split2(x):
    hi = x.astype(jnp.bfloat16)
    return hi, (x - hi.astype(jnp.float32)).astype(jnp.bfloat16)


def dot3(a, b):
    f32 = jnp.float32
    return (
        jnp.dot(a[0], b[0], preferred_element_type=f32)
        + jnp.dot(a[0], b[1], preferred_element_type=f32)
        + jnp.dot(a[1], b[0], preferred_element_type=f32)
    )


def add_project_kernel(slot_ref, g_ref, m_ref, b_ref, s_ref, *refs):
    hi_ref, lo_ref = refs[8:]

    @pl.when(pl.program_id(0) == 0)
    def _():
        hi_ref[...], lo_ref[...] = split2(b_ref[...])

    rows, cols = m_ref.shape
    grad = [unpack(g_ref[k], rows // 4, cols) for k in range(4)]
    summed = m_ref[...] + jnp.concatenate(grad, 0).astype(jnp.float32)
    s_ref[...] = summed
    part = dot3(split2(summed), (hi_ref[...], lo_ref[...]))
    half = part.shape[1] // 2
    for side in range(2):
        slot = slot_ref[4 * side + pl.program_id(0)]
        for to in range(4):

            @pl.when(slot == to)
            def _(side=side, to=to):
                refs[4 * side + to][...] = part[:, side * half : (side + 1) * half]


def add_project(slots, grad, momentum, basis):
    rows, cols = momentum.shape
    rank = basis.shape[1]
    step = rows // 4
    return pl.pallas_call(
        add_project_kernel,
        grid=(rows // step,),
        in_specs=[
            pl.BlockSpec(memory_space=pltpu.SMEM),
            pl.BlockSpec((4,) + grad.shape[1:], lambda i: (i, 0, 0)),
            pl.BlockSpec((step, cols), lambda i: (i, 0)),
            pl.BlockSpec((cols, rank), lambda i: (0, 0)),
        ],
        out_specs=[
            pl.BlockSpec((step, cols), lambda i: (i, 0)),
        ]
        + [pl.BlockSpec((step, rank // 2), lambda i: (0, 0))] * 8,
        out_shape=[jax.ShapeDtypeStruct((rows, cols), jnp.float32)]
        + [jax.ShapeDtypeStruct((step, rank // 2), jnp.float32)] * 8,
        scratch_shapes=[pltpu.VMEM((cols, rank), jnp.bfloat16)] * 2,
        compiler_params=pltpu.CompilerParams(vmem_limit_bytes=36 * 1024 * 1024),
        cost_estimate=pl.CostEstimate(
            flops=6 * rows * cols * rank, bytes_accessed=10 * rows * cols, transcendentals=0
        ),
        name="add_project",
    )(slots, grad, momentum, basis)


def parts_kernel(x_ref, hi_ref, lo_ref):
    hi_ref[...], lo_ref[...] = split2(x_ref[...])


def parts_of(x):
    vmem = pl.BlockSpec(memory_space=pltpu.VMEM)
    return pl.pallas_call(
        parts_kernel,
        in_specs=[vmem],
        out_specs=[vmem, vmem],
        out_shape=[jax.ShapeDtypeStruct(x.shape, jnp.bfloat16)] * 2,
        compiler_params=pltpu.CompilerParams(vmem_limit_bytes=16 * 1024 * 1024),
        cost_estimate=pl.CostEstimate(
            flops=2 * x.size, bytes_accessed=8 * x.size, transcendentals=0
        ),
        name="parts",
    )(x)


def update_kernel(q_ref, scale_ref, hi_ref, lo_ref, o_ref):
    q = split2(q_ref[...] * scale_ref[...])
    dims = (((1,), (1,)), ((), ()))
    f32 = jnp.float32
    out = lax.dot_general(q[0], hi_ref[...], dims, preferred_element_type=f32)
    out += lax.dot_general(q[0], lo_ref[...], dims, preferred_element_type=f32)
    out += lax.dot_general(q[1], hi_ref[...], dims, preferred_element_type=f32)
    out = out.astype(jnp.bfloat16)
    part = out.shape[0] // 4
    for k in range(4):
        o_ref[k] = pack(out[k * part : (k + 1) * part])


def update_of(orthonormal, scale, parts):
    rows, rank = orthonormal.shape
    cols = parts[0].shape[0]
    step = rows // 4
    packed = packed_rows(rows // 16, cols)
    whole = pl.BlockSpec((cols, rank), lambda i: (0, 0))
    return pl.pallas_call(
        update_kernel,
        grid=(4,),
        in_specs=[
            pl.BlockSpec((step, rank), lambda i: (i, 0)),
            pl.BlockSpec((1, rank), lambda i: (0, 0)),
            whole,
            whole,
        ],
        out_specs=pl.BlockSpec((4, packed, 128), lambda i: (i, 0, 0)),
        out_shape=jax.ShapeDtypeStruct((16, packed, 128), jnp.bfloat16),
        compiler_params=pltpu.CompilerParams(vmem_limit_bytes=32 * 1024 * 1024),
        cost_estimate=pl.CostEstimate(
            flops=6 * rows * cols * rank, bytes_accessed=4 * rows * cols, transcendentals=0
        ),
        name="update_tile",
    )(orthonormal, scale, *parts)


def other_core(x):
    return lax.ppermute(x, "c", [(0, 1), (1, 0)])


def partners(axis):
    i = lax.axis_index(axis)
    first = lax.axis_index("c") == 0
    one, two = jnp.bitwise_xor(i, 1), 3 - i
    return i, jnp.where(first, one, two), jnp.where(first, two, one), jnp.bitwise_xor(i, 2)


def swap(x, axis, turn):
    perm = []
    for c in range(2):
        for i in range(4):
            j = i ^ 1 if c == turn else 3 - i
            perm.append((2 * i + c, 2 * j + c) if axis == "y" else (4 * c + i, 4 * c + j))
    return lax.ppermute(x, ("y", "c") if axis == "y" else ("c", axis), perm)


def pick(x, i):
    return lax.dynamic_index_in_dim(x, i, 0, False)


def slots_of(axis):
    i, p1, p2, far = partners(axis)
    k = jnp.arange(4, dtype=jnp.int32)
    return jnp.where(k == i, 0, jnp.where(k == p2, 1, jnp.where(k == p1, 2, 3))).astype(jnp.int32)


def pair_scatter_start(parts, axis):
    got_far = swap(parts[3], axis, 0)
    got_own = swap(parts[2], axis, 0)
    return parts[0], got_own, swap(parts[1] + got_far, axis, 1)


def pair_scatter(parts, axis):
    return sum_parts(pair_scatter_start(parts, axis))


def sum_parts(parts):
    return parts[0] + parts[1] + parts[2]


def quarters(x, axis):
    i, p1, p2, far = partners(axis)
    return [pick(x, k) for k in (i, p2, p1, far)]


def pair_gather_start(x, axis):
    return x, swap(x, axis, 1), swap(x, axis, 0)


def place(parts, axis):
    i, p1, p2, far = partners(axis)
    out = jnp.zeros((4,) + parts[0].shape, parts[0].dtype)
    for where, part in zip((i, p2, p1, far), parts):
        out = lax.dynamic_update_index_in_dim(out, part, where, 0)
    return out


def pair_gather_parts(x, axis):
    parts = pair_gather_start(x, axis)
    return (*parts, swap(parts[1], axis, 0))


def pair_sum(x, axis):
    x = x + swap(x, axis, 0)
    return x + swap(x, axis, 1)


def flip(x, axis, d):
    return lax.ppermute(x, axis, [(i, i ^ d) for i in range(4)])


def direct_gather(x, axis):
    me = lax.axis_index(axis)
    out = jnp.zeros((4,) + x.shape, x.dtype)
    for d, part in enumerate((x, flip(x, axis, 1), flip(x, axis, 2), flip(x, axis, 3))):
        out = lax.dynamic_update_index_in_dim(out, part, jnp.bitwise_xor(me, d), 0)
    return out


def direct_sum(x, axis):
    return (x + flip(x, axis, 2)) + (flip(x, axis, 1) + flip(x, axis, 3))


def arrange_kernel(place_ref, *refs):
    o_ref = refs[8]
    rows, cols = refs[0].shape
    for side in range(2):
        for k in range(4):
            row = pl.multiple_of(place_ref[4 * side + k] * rows, rows)
            o_ref[pl.ds(row, rows), side * cols : (side + 1) * cols] = refs[4 * side + k][...]


def arrange(places, left, right):
    rows, cols = left[0].shape
    return pl.pallas_call(
        arrange_kernel,
        in_specs=[pl.BlockSpec(memory_space=pltpu.SMEM)]
        + [pl.BlockSpec(memory_space=pltpu.VMEM)] * 8,
        out_specs=pl.BlockSpec(memory_space=pltpu.VMEM),
        out_shape=jax.ShapeDtypeStruct((4 * rows, 2 * cols), jnp.float32),
        compiler_params=pltpu.CompilerParams(vmem_limit_bytes=16 * 1024 * 1024),
        cost_estimate=pl.CostEstimate(
            flops=0, bytes_accessed=64 * rows * cols, transcendentals=0
        ),
        name="arrange",
    )(places, *left, *right)


def reduce_projected(left, right):
    a, b = pair_scatter(left, "z"), pair_scatter(right, "x")
    a, b = pair_sum(a, "x"), pair_sum(b, "z")
    places = []
    for axis in ("z", "x"):
        i, p1, p2, far = partners(axis)
        places += [i, p2, p1, far]
    return arrange(
        jnp.stack(places).astype(jnp.int32), pair_gather_parts(a, "z"), pair_gather_parts(b, "x")
    )


def both_halves(mine):
    first = lax.axis_index("c") == 0
    theirs = other_core(mine)
    return jnp.concatenate([jnp.where(first, mine, theirs), jnp.where(first, theirs, mine)], 1)


def core_scatter(x):
    first = lax.axis_index("c") == 0
    left, right = jnp.split(x, 2, axis=1)
    return jnp.where(first, left, right) + other_core(jnp.where(first, right, left))


def gram_slab(projected):
    slab = projected.shape[1] // 4
    mine = lax.dynamic_slice_in_dim(projected, lax.axis_index("z") * slab, slab, 1)
    return lax.dot_general(mine, projected, (((0,), (0,)), ((), ())), precision=HIGHEST)


def gram_gather(part):
    n = 4 * part.shape[0]
    return both_halves(direct_gather(part, "z").reshape(n, n // 2))


def local(gradient, momentum, basis):
    rows, cols = momentum.shape
    pieces = lax.all_to_all(cut_columns(gradient, 16), ("z", "x"), 0, 0, tiled=True)
    slots = jnp.concatenate([slots_of("z"), slots_of("x")])
    summed, *partial = add_project(slots, pieces, momentum, basis)
    projected = reduce_projected(partial[:4], partial[4:])
    slab = gram_slab(projected)
    dims = (((0,), (0,)), ((), ()))
    half = RANK // 2
    stages = (
        (core_scatter, lambda p: lax.dot_general(summed, p, dims, precision=HIGH)),
        (
            lambda g: direct_sum(g, "y"),
            lambda w: core_scatter(jnp.pad(w, ((0, -cols % 32), (0, 0)))),
        ),
        (gram_gather, lambda w: pair_scatter(quarters(w.reshape(4, -1, half), "y"), "y")),
        (lambda g: inverse_step(g, 0), lambda w: pair_gather_start(w, "y")),
        (lambda g: inverse_step(g, 1), lambda w: (*w, swap(w[1], "y", 0))),
        (lambda g: inverse_step(g, 2), lambda w: place(w, "y")),
        (lambda g: inverse_step(g, 3), lambda w: both_halves(w.reshape(-1, half))),
    )
    mixed = projected
    inverse = slab
    for of_gram, of_mixed in stages:
        inverse, mixed = lax.optimization_barrier((inverse, mixed))
        inverse, mixed = of_gram(inverse), of_mixed(mixed)
    mixed = mixed[:cols]
    contract = (((1,), (1,)), ((), ()))
    orthonormal = lax.dot_general(projected, inverse, contract, precision=HIGH)
    right_factor = lax.dot_general(mixed, inverse, contract, precision=HIGH)
    squares = jnp.sum(right_factor * right_factor, axis=0, keepdims=True)
    squares = direct_sum(jnp.broadcast_to(squares, (8, RANK)), "z")
    parts = parts_of(right_factor)
    squares = direct_sum(squares, "x")[:1]
    inverse_norm = lax.rsqrt(squares + epsilon)
    scaling = (D * FF / RANK) ** 0.5
    update_tile = update_of(orthonormal, scaling * inverse_norm, parts)
    pieces = lax.all_to_all(update_tile, ("z", "x"), 0, 0, tiled=True)
    right_factor, _ = lax.optimization_barrier((right_factor, update_tile))
    new_basis = right_factor * inverse_norm
    new_momentum = summed - feedback_keep * lax.dot_general(
        orthonormal, right_factor, contract, precision=HIGH
    )
    return (join_columns(pieces, rows // 16, cols), new_momentum, new_basis)


def solution(mesh):
    fine = Mesh(mesh.devices.reshape(4, 2, 4, 4), ("y", "c", "z", "x"))
    row, col = ("y", "c"), ("z", "x")
    return jax.shard_map(
        local,
        mesh=fine,
        in_specs=(P(row + col, None), P(row, col), P(col, None)),
        out_specs=(P(row + col, None), P(row, col), P(col, None)),
        check_vma=False,
    )
```
